128 devices in a mesh: axial: 8 (over y, core), azim: 16 (over z, x).
Axes of the slice: x: 4, y: 4, z: 4, core: 2. Of those that a mesh axis runs over, the one named last changes fastest.
Arguments:
- surface_pos: float32 [3, 131072], P(None, ('axial', 'azim')), may hold values from 0 to 1
- surface_coef: float32 [3, 131072], P(None, ('axial', 'azim')), may hold values from -3 to 3
- send_rows: int32 [128, 512], P(('axial', 'azim')), may hold values from 0 to 1023
- volume_pos: float32 [3, 8388608], P(None, ('axial', 'azim')), may hold values from 0 to 1
- relay_order: int32 [128, 65536], P(('axial', 'azim')), may hold values from 0 to 65535, each once within a row
- block_cols: int32 [16384, 8], P(('axial', 'azim')), may hold values from 0 to 511, as said below
- block_count: int32 [16384], P(('axial', 'azim')), may hold values from 1 to 8
Outputs:
- displacement: float32 [3, 8388608], P(None, ('axial', 'azim'))
The draws below stay inside these ranges and needn't reach their ends.
Inputs may be any that keep to these rules, and one draw needn't show every extreme that they name: `block_cols`: A row block on axial slab a lists only center blocks owned by slabs a - 1, a, a + 1; some row block lists 8 live entries.
All inputs are finite; a program needn't handle non-finite values.
Results may differ from the reference program's by a relative error of at most 0.0003.
Values sent between devices are 32-bit elements; how exact they have to be, the bound alone decides.
No kernel may reach another device: no remote copies, remote signals or barrier semaphores. Data moves between devices by JAX's collectives and lax.ppermute only.
A program may use at most 192 MiB of HBM per device.

```python
import jax
import jax.numpy as jnp
from jax import lax

S_DEV = 1024
V_DEV = 65536
C_DEV = 512
CB = 128
RB = 512
K_MAX = 8
GROUP = 8
NS = 131072
NV = 8388608
N_AXIAL = 8
N_AZIM = 16
DEVICES = 128


def draw_block_count(key, part):
    nrb_device = V_DEV // RB
    ndevices = N_AXIAL * N_AZIM
    highest = jax.random.randint(jax.random.fold_in(key, 11), (ndevices,), 1, K_MAX + 1)
    highest = highest.at[0].set(K_MAX)
    raw = jax.random.randint(jax.random.fold_in(key, 12), (ndevices, nrb_device), 0, 1 << 20)
    counts = raw % highest[:, None] + 1
    counts = counts.at[:, 0].set(highest)
    return counts.reshape(-1).astype(jnp.int32)


def draw_block_cols(key, part):
    nrb_device = V_DEV // RB
    ndevices = N_AXIAL * N_AZIM
    per_slab = N_AZIM * C_DEV // CB
    axial = jnp.arange(ndevices, dtype=jnp.int32) // N_AZIM
    lowest = jnp.maximum(axial - 1, 0) * per_slab
    upper = (jnp.minimum(axial + 1, N_AXIAL - 1) + 1) * per_slab
    raw = jax.random.randint(jax.random.fold_in(key, 13), (ndevices, nrb_device, K_MAX), 0, 1 << 24)
    chosen = lowest[:, None, None] + raw % (upper - lowest)[:, None, None]
    return chosen.reshape(ndevices * nrb_device, K_MAX).astype(jnp.int32)


def place_ends(values, rng, least, high):
    longest = values.shape.index(max(values.shape))
    spots = []
    for shift in (0, 1):
        where = [jax.random.randint(jax.random.fold_in(rng, axis), (), 0, length) for axis, length in enumerate(values.shape)]
        where[longest] = (where[longest] + shift) % values.shape[longest]
        spots.append(tuple(where))
    return values.at[spots[0]].set(least).at[spots[1]].set(high)


def shard_levels(rng, dims, pieces, smallest, high):
    def one(position, shards_of):
        draws = jax.random.uniform(jax.random.fold_in(jax.random.fold_in(rng, 6), position), (shards_of,), jnp.float32, smallest / len(pieces), high / len(pieces))
        return jnp.repeat(jnp.exp(draws), dims[position] // shards_of).reshape((-1,) + (1,) * (len(dims) - position - 1))

    level = one(*pieces[0])
    for cut in pieces[1:]:
        level = level * one(*cut)
    return level


def bell_draw(stream_key, dims, spread, bound, pieces=(), held_as=jnp.bfloat16):
    entries = jax.random.normal(stream_key, dims, jnp.float32) * spread
    if len(pieces) > 0:
        entries = shard_levels(stream_key, dims, pieces, -0.22, 0.18) * entries
    return jnp.clip(entries, min=-bound, max=bound).astype(held_as)


def setup_inputs(seed: int = 0) -> dict:
    arg_keys = jax.random.split(jax.random.key(seed), 8)
    surface_pos = jnp.clip(1.0 * jax.random.uniform(arg_keys[0], (3, NS), jnp.float32) ** shard_levels(arg_keys[0], (3, NS), ((1, 128),), -0.2, 0.2), 0.0, 1.0)
    surface_coef = bell_draw(arg_keys[1], (3, NS), 0.5, 3.0, ((1, 128),), jnp.float32)
    send_rows = place_ends(jax.random.randint(arg_keys[2], (DEVICES, C_DEV), 0, S_DEV), jax.random.fold_in(arg_keys[2], 1), 0, S_DEV - 1).astype(jnp.int32)
    volume_pos = jnp.clip(1.0 * jax.random.uniform(arg_keys[3], (3, NV), jnp.float32) ** shard_levels(arg_keys[3], (3, NV), ((1, 128),), -0.2, 0.2), 0.0, 1.0)
    relay_order = jax.vmap(lambda own: jax.random.permutation(own, V_DEV))(jax.random.split(arg_keys[4], DEVICES)).reshape((DEVICES, V_DEV)).astype(jnp.int32)
    block_cols = draw_block_cols(jax.random.fold_in(arg_keys[7], 71), 0)
    block_count = draw_block_count(jax.random.fold_in(arg_keys[7], 71), 0)
    return dict(surface_pos=surface_pos, surface_coef=surface_coef, send_rows=send_rows, volume_pos=volume_pos, relay_order=relay_order, block_cols=block_cols, block_count=block_count)


support_radius = 0.5

def evaluate(rows, columns, counts, table, offset):
    nrb = columns.shape[0]
    size = rows.shape[1] // nrb
    blocks = table.reshape(6, -1, CB)

    def one_group(group_index):
        start = group_index * GROUP
        points = lax.dynamic_slice_in_dim(rows, start * size, GROUP * size, 1).reshape(3, GROUP, size)
        chosen_ids = lax.dynamic_slice_in_dim(columns, start, GROUP, 0) - offset
        live = lax.dynamic_slice_in_dim(counts, start, GROUP, 0)

        def add_block(step, total):
            chosen = jnp.take(blocks, chosen_ids[:, step], axis=1)
            diff = points[:, :, :, None] - chosen[0:3, :, None, :]
            dist = jnp.sqrt(lax.optimization_barrier(jnp.sum(diff * diff, axis=0))) / support_radius
            nearer = jnp.maximum(1.0 - dist, 0.0)
            kernel = nearer * nearer * nearer * nearer * (4.0 * dist + 1.0)
            weight = jnp.where((step < live)[:, None, None], kernel, 0.0)
            return total + jnp.einsum('grc,dgc->dgr', weight, chosen[3:6], precision=lax.Precision.HIGHEST)
        return lax.fori_loop(jnp.int32(0), jnp.max(live), add_block, jnp.zeros((3, GROUP, size), jnp.float32))
    result = lax.map(one_group, jnp.arange(nrb // GROUP, dtype=jnp.int32))
    return jnp.moveaxis(result, 0, 1).reshape(3, -1)

def reference(surface_pos, surface_coef, send_rows, volume_pos, relay_order, block_cols, block_count):
    ndevices = N_AXIAL * N_AZIM
    per_owner = C_DEV // ndevices
    surface = jnp.concatenate([surface_pos, surface_coef], 0)
    lists = send_rows.reshape(ndevices, ndevices, per_owner)
    source = (jnp.arange(ndevices, dtype=jnp.int32) * S_DEV)[None, :, None]
    index = (jnp.transpose(lists, (1, 0, 2)) + source).reshape(-1).astype(jnp.int32)
    table = jnp.take(surface, index, axis=1)
    local = volume_pos.reshape(3, ndevices, V_DEV)
    permuted = jnp.take_along_axis(local, relay_order[None].astype(jnp.int32), axis=2)
    piece = V_DEV // N_AZIM
    kernel = permuted.reshape(3, N_AXIAL, N_AZIM, N_AZIM, piece).transpose(0, 1, 3, 2, 4).reshape(3, -1)
    field = evaluate(kernel, block_cols, block_count, table, 0)
    back = field.reshape(3, N_AXIAL, N_AZIM, N_AZIM, piece).transpose(0, 1, 3, 2, 4).reshape(3, ndevices, V_DEV)
    inverse = jnp.argsort(relay_order, axis=1).astype(jnp.int32)
    return jnp.take_along_axis(back, inverse[None], axis=2).reshape(3, -1)
```

```python
import functools
import jax
import jax.numpy as jnp
from jax import lax
from jax.experimental import pallas as pl
from jax.experimental.pallas import tpu as pltpu
from jax.sharding import PartitionSpec as P

F32 = jnp.float32
BF16 = jnp.bfloat16
LANES = 128
CHUNK = 4096
SLOTS = 4
BATCH = 1024


def pieces(value, count):
    out = []
    for _ in range(count):
        part = value.astype(BF16).astype(F32)
        out.append(part)
        value = value - part
    return out


def build_rows(pos_ref, rows):
    def build(step, carry):
        start = pl.multiple_of(step * 512, 512)
        x = pos_ref[:, pl.ds(start, 512)] * 2.0 - 1.0
        x1, x2 = pieces(x, 2)
        held = x1 + x2
        n1, n2, n3 = pieces(jnp.sum(held * held, axis=0, keepdims=True), 3)
        one, zero = jnp.ones_like(n1), jnp.zeros_like(n1)
        v1 = jnp.concatenate([x1, n1, one, n3, one, zero], 0)
        v2 = jnp.concatenate([x2, n2, zero, zero, zero, zero], 0)
        stacked = jnp.concatenate(
            [v[:, g * LANES : (g + 1) * LANES] for g in range(4) for v in (v1, v1, v2, v2)], 0
        )
        dense = stacked.T
        for g in range(4):
            turned = dense if g == 0 else pltpu.roll(dense, LANES - 32 * g, 1)
            rows[pl.ds(start + g * LANES, LANES), :] = turned
        return carry

    lax.fori_loop(0, pos_ref.shape[1] // 512, build, 0, unroll=2)


def gather_kernel(order_ref, pos_ref, out_ref, rows, *rest):
    ids, sems = rest[:SLOTS], rest[SLOTS]
    step, steps = pl.program_id(0), pl.num_programs(0)

    def fetch(at, slot):
        source = order_ref.at[pl.ds(at * CHUNK + slot * BATCH, BATCH)]
        return pltpu.make_async_copy(source, ids[slot], sems.at[slot])

    @pl.when(step == 0)
    def _():
        for slot in range(SLOTS):
            fetch(0, slot).start()
        build_rows(pos_ref, rows)

    for slot in range(SLOTS):
        fetch(step, slot).wait()
        for k in range(BATCH):
            out_ref[pl.ds(slot * BATCH + k, 1), :] = rows[pl.ds(ids[slot][k], 1), :]

        @pl.when(step + 1 < steps)
        def _():
            fetch(step + 1, slot).start()


def gather_rows(order, pos):
    nodes = pos.shape[1]
    return pl.pallas_call(
        gather_kernel,
        grid=(nodes // CHUNK,),
        in_specs=[
            pl.BlockSpec(memory_space=pl.ANY),
            pl.BlockSpec((3, nodes), lambda i: (0, 0)),
        ],
        out_specs=pl.BlockSpec((CHUNK, LANES), lambda i: (i, 0)),
        out_shape=jax.ShapeDtypeStruct((nodes, LANES), F32),
        scratch_shapes=[pltpu.VMEM((nodes, LANES), F32)]
        + [pltpu.SMEM((BATCH,), jnp.int32) for _ in range(SLOTS)]
        + [pltpu.SemaphoreType.DMA((SLOTS,))],
        compiler_params=pltpu.CompilerParams(vmem_limit_bytes=58 * 2**20),
        cost_estimate=pl.CostEstimate(flops=10**9, bytes_accessed=100 * 2**20, transcendentals=0),
        name="gather_rows",
    )(order, pos)


IDS = 4


def segments(width):
    return lax.broadcasted_iota(jnp.int32, (1, LANES), 1) // width


def read_lists(where_ref, sent_ref, cols, counts, cols_smem, counts_smem, sem):
    azim = counts.shape[0]
    mine = where_ref[0] * azim
    for k in range(azim):
        listed = sent_ref[mine + k, 24:32, :]
        cols[k * 8 : (k + 1) * 8, :] = listed.astype(jnp.int32)
        live = jnp.where(listed >= 0.0, 1.0, 0.0)
        counts[k : k + 1, :] = jnp.sum(live, axis=0, keepdims=True).astype(jnp.int32)
    first = pltpu.make_async_copy(cols, cols_smem, sem.at[0])
    second = pltpu.make_async_copy(counts, counts_smem, sem.at[1])
    first.start()
    second.start()
    return first, second


def build_table(base, sent_ref, turned, table):
    for row in range(24):
        turned[row] = sent_ref[:, row, :].T
    owners = 48
    segment = segments(32)
    for q in range(4):
        comps = []
        for c in range(6):
            value = None
            for k in range(4):
                part = turned[c * 4 + k, pl.ds(base, owners), :]
                if k != q:
                    part = pltpu.roll(part, (32 * (k - q)) % LANES, 1)
                value = part if value is None else jnp.where(segment == k, part, value)
            comps.append(value)
        first, second, total = [], [], None
        for c in range(3):
            c1, c2 = pieces(comps[c] * 2.0 - 1.0, 2)
            held = c1 + c2
            total = held * held if total is None else total + held * held
            first.append(-2.0 * c1)
            second.append(-2.0 * c2)
        m1, m2, m3 = pieces(total, 3)
        one, zero = jnp.ones_like(m1), jnp.zeros_like(m1)
        high, low = [], []
        for c in range(3):
            h, l = pieces(4.0 * comps[3 + c], 2)
            high.append(h)
            low.append(l)
        rows = first + [one, m1, one, m3, zero]
        rows += second + [zero, m2, zero, zero, zero]
        rows += high + low + [zero, zero]
        for f, value in enumerate(rows):
            table[pl.ds(q * 24 + f, owners, stride=96), :] = value


def add_center_block(points, listed, total, fresh, extra=None):
    features = jnp.concatenate([listed[0:16], listed[0:16]], 0).astype(BF16)
    coefs = jnp.concatenate([listed[16:24], listed[16:24]], 1).astype(BF16)
    for part in range(4):
        at = pl.ds(part * LANES, LANES)
        square = jnp.dot(points[at, :], features, preferred_element_type=F32)
        square = jnp.minimum(jnp.maximum(square, 1e-12), 1.0)
        left = 1.0 - square * lax.rsqrt(square)
        twice = left * left
        weight = (twice * twice) * (1.25 - left)
        high = weight.astype(BF16)
        low = (weight - high.astype(F32)).astype(BF16)
        added = lax.dot_general(
            jnp.concatenate([high, low], 1),
            coefs,
            (((1,), (1,)), ((), ())),
            preferred_element_type=F32,
        )
        total[at, 0:8] = added if fresh else total[at, 0:8] + added
        if extra is not None:
            extra(part)


def evaluate_kernel(where_ref, sent_ref, order_ref, rows_ref, out_ref, *scratch):
    placed, turned, table, points, totals, cols, counts, cols_smem, counts_smem = scratch[:9]
    ids, sems, list_sem = scratch[9 : 9 + IDS], scratch[9 + IDS], scratch[10 + IDS]
    step, steps = pl.program_id(0), pl.num_programs(0)
    per_step = CHUNK // 512
    block_total = steps * per_step
    offset = where_ref[3]

    def fetch(block, slot):
        source = order_ref.at[pl.ds(pl.multiple_of(block * 512, 512), 512)]
        return pltpu.make_async_copy(source, ids[slot], sems.at[slot])

    @pl.when(step == 0)
    def _():
        fetch(0, IDS - 1).start()
        waits = read_lists(where_ref, sent_ref, cols, counts, cols_smem, counts_smem, list_sem)
        build_table(pl.multiple_of(offset, 16), sent_ref, turned, table)
        for wait in waits:
            wait.wait()
        for slot in range(IDS - 2):
            fetch(slot, slot).start()

    def place(slot, part, parts=4):
        size = 512 // parts
        for k in range(part * size, (part + 1) * size):
            placed[pl.ds(ids[slot][k], 1), :] = totals[slot % 2, pl.ds(k, 1), :]

    def four_blocks(half, carry):
        for slot in range(IDS):
            inner = half * IDS + slot
            block = step * per_step + inner
            before = (slot - 1) % IDS
            total = totals.at[slot % 2]
            lane = where_ref[1] * 8 + inner
            points[...] = rows_ref[pl.ds(pl.multiple_of(inner * 512, 512), 512), 0:32].astype(BF16)
            fetch(0, before).wait()

            def listed(j):
                chosen = cols_smem[step * 8 + j, lane] - offset * 4
                return table[pl.ds(pl.multiple_of(chosen * 24, 8), 24), :]

            add_center_block(points, listed(0), total, True, functools.partial(place, before))

            @pl.when(block + 2 < block_total)
            def _():
                fetch(block + 2, (slot + 2) % IDS).start()

            def one_block(j, carry):
                add_center_block(points, listed(j), total, False)
                return carry

            lax.fori_loop(1, counts_smem[step, lane], one_block, 0)
        return carry

    lax.fori_loop(0, per_step // IDS, four_blocks, 0)

    @pl.when(step == steps - 1)
    def _():
        fetch(0, IDS - 1).wait()
        place(IDS - 1, 0, 1)
        segment = segments(8)

        def close(group, carry):
            start = pl.multiple_of(group * 2048, 2048)
            dense = placed[pl.ds(start, LANES), :]
            for g in range(1, 16):
                part = pltpu.roll(placed[pl.ds(start + g * LANES, LANES), :], 8 * g, 1)
                dense = jnp.where(segment == g, part, dense)
            flat = dense.T
            for g in range(16):
                result = flat[8 * g : 8 * g + 3] + flat[8 * g + 3 : 8 * g + 6]
                out_ref[:, pl.ds(start + g * LANES, LANES)] = result
            return carry

        lax.fori_loop(0, out_ref.shape[1] // 2048, close, 0)


def evaluate_rows(where, sent, order, rows):
    nodes = rows.shape[0]
    vmem = pl.BlockSpec(memory_space=pltpu.VMEM)
    return pl.pallas_call(
        evaluate_kernel,
        grid=(nodes // CHUNK,),
        in_specs=[
            pl.BlockSpec(memory_space=pltpu.SMEM),
            vmem,
            pl.BlockSpec(memory_space=pl.ANY),
            pl.BlockSpec((CHUNK, LANES), lambda i: (i, 0)),
        ],
        out_specs=vmem,
        out_shape=jax.ShapeDtypeStruct((3, nodes), F32),
        scratch_shapes=[
            pltpu.VMEM((nodes, LANES), F32),
            pltpu.VMEM((24, LANES, LANES), F32),
            pltpu.VMEM((192 * 24, LANES), F32),
            pltpu.VMEM((512, 32), BF16),
            pltpu.VMEM((2, 512, LANES), F32),
            pltpu.VMEM((LANES, LANES), jnp.int32),
            pltpu.VMEM((16, LANES), jnp.int32),
            pltpu.SMEM((LANES, LANES), jnp.int32),
            pltpu.SMEM((16, LANES), jnp.int32),
        ]
        + [pltpu.SMEM((512,), jnp.int32) for _ in range(IDS)]
        + [pltpu.SemaphoreType.DMA((IDS,)), pltpu.SemaphoreType.DMA((2,))],
        compiler_params=pltpu.CompilerParams(vmem_limit_bytes=58 * 2**20),
        cost_estimate=pl.CostEstimate(flops=10**10, bytes_accessed=100 * 2**20, transcendentals=0),
        name="evaluate_rows",
    )(where, sent, order, rows)


def per_device(
    surface_pos, surface_coef, send_rows, volume_pos, relay_order, block_cols, block_count
):
    axial, azim = lax.axis_index("axial"), lax.axis_index("azim")
    slabs, sectors = lax.axis_size("axial"), lax.axis_size("azim")
    surface = jnp.concatenate([surface_pos, surface_coef], 0)
    picked = send_rows[0].reshape(-1, 4).T.reshape(-1)
    outgoing = surface.at[:, picked].get(mode="promise_in_bounds").reshape(24, -1)
    alive = jnp.arange(8, dtype=jnp.int32)[:, None] < block_count[None, :]
    listed = jnp.where(alive, block_cols.T, -1).astype(F32)
    payload = jnp.concatenate([outgoing, listed], 0)
    sent = lax.all_gather(payload, ("axial", "azim"), axis=0, tiled=False)
    order = relay_order[0]
    rows = gather_rows(order, volume_pos)
    low = jnp.clip((axial - 1) * sectors, 0, (slabs - 3) * sectors)
    where = jnp.stack([axial, azim, jnp.int32(slabs), low]).astype(jnp.int32)
    return evaluate_rows(where, sent, order, rows)


def solution(mesh):
    placed = (
        P(None, ("axial", "azim")),
        P(None, ("axial", "azim")),
        P(("axial", "azim"), None),
        P(None, ("axial", "azim")),
        P(("axial", "azim"), None),
        P(("axial", "azim"), None),
        P(("axial", "azim")),
    )
    return jax.shard_map(
        per_device,
        mesh=mesh,
        in_specs=placed,
        out_specs=P(None, ("axial", "azim")),
        check_vma=False,
    )
```

```python
import functools
import jax
import jax.numpy as jnp
from jax import lax
from jax.experimental import pallas as pl
from jax.experimental.pallas import tpu as pltpu
from jax.sharding import PartitionSpec as P

F32 = jnp.float32
BF16 = jnp.bfloat16
LANES = 128
CHUNK = 4096
SLOTS = 4
BATCH = 1024


def pieces(value, count):
    out = []
    for _ in range(count):
        part = value.astype(BF16).astype(F32)
        out.append(part)
        value = value - part
    return out


def build_rows(pos_ref, rows):
    def build(step, carry):
        start = pl.multiple_of(step * 512, 512)
        x = pos_ref[:, pl.ds(start, 512)] * 2.0 - 1.0
        x1, x2 = pieces(x, 2)
        held = x1 + x2
        n1, n2, n3 = pieces(jnp.sum(held * held, axis=0, keepdims=True), 3)
        one, zero = jnp.ones_like(n1), jnp.zeros_like(n1)
        v1 = jnp.concatenate([x1, n1, one, n3, one, zero], 0)
        v2 = jnp.concatenate([x2, n2, zero, zero, zero, zero], 0)
        stacked = jnp.concatenate(
            [v[:, g * LANES : (g + 1) * LANES] for g in range(4) for v in (v1, v1, v2, v2)], 0
        )
        dense = stacked.T
        for g in range(4):
            turned = dense if g == 0 else pltpu.roll(dense, LANES - 32 * g, 1)
            rows[pl.ds(start + g * LANES, LANES), :] = turned
        return carry

    lax.fori_loop(0, pos_ref.shape[1] // 512, build, 0, unroll=4)


def gather_kernel(order_ref, pos_ref, out_ref, rows, *rest):
    taken, ids, sems = rest[:2], rest[2 : 2 + SLOTS], rest[2 + SLOTS]
    steps = pos_ref.shape[1] // CHUNK

    def fetch(step, slot):
        start = pl.multiple_of(step * CHUNK + slot * BATCH, BATCH)
        source = order_ref.at[pl.ds(start, BATCH)]
        return pltpu.make_async_copy(source, ids[slot], sems.at[slot])

    def turn(held, start):
        for part in range(BATCH // LANES):
            flat = held[part * LANES : (part + 1) * LANES, :].T
            at = pl.ds(pl.multiple_of(start + part * LANES, LANES), LANES)
            out_ref[:, at] = flat[0:32].astype(BF16)

    for slot in range(SLOTS):
        fetch(0, slot).start()
    build_rows(pos_ref, rows)

    def one_step(step, carry):
        for slot in range(SLOTS):
            fetch(step, slot).wait()
            for k in range(BATCH):
                taken[slot % 2][pl.ds(k, 1), :] = rows[pl.ds(ids[slot][k], 1), :]
            turn(taken[1 - slot % 2], jnp.maximum(step * CHUNK + (slot - 1) * BATCH, 0))

            @pl.when(step + 1 < steps)
            def _():
                fetch(step + 1, slot).start()

        return carry

    lax.fori_loop(0, steps, one_step, 0)
    turn(taken[(SLOTS - 1) % 2], steps * CHUNK - BATCH)


def gather_rows(order, pos):
    nodes = pos.shape[1]
    vmem = pl.BlockSpec(memory_space=pltpu.VMEM)
    return pl.pallas_call(
        gather_kernel,
        in_specs=[pl.BlockSpec(memory_space=pl.ANY), vmem],
        out_specs=vmem,
        out_shape=jax.ShapeDtypeStruct((32, nodes), BF16),
        scratch_shapes=[pltpu.VMEM((nodes, LANES), F32)]
        + [pltpu.VMEM((BATCH, LANES), F32) for _ in range(2)]
        + [pltpu.SMEM((BATCH,), jnp.int32) for _ in range(SLOTS)]
        + [pltpu.SemaphoreType.DMA((SLOTS,))],
        compiler_params=pltpu.CompilerParams(vmem_limit_bytes=58 * 2**20),
        cost_estimate=pl.CostEstimate(flops=10**9, bytes_accessed=100 * 2**20, transcendentals=0),
        name="gather_rows",
    )(order, pos)


IDS = 4


def segments(width):
    return lax.broadcasted_iota(jnp.int32, (1, LANES), 1) // width


def read_lists(where_ref, sent_ref, cols, counts, cols_smem, counts_smem, sem):
    azim = counts.shape[0]
    mine = where_ref[0] * azim
    for k in range(azim):
        listed = sent_ref[mine + k, 24:32, :]
        cols[k * 8 : (k + 1) * 8, :] = listed.astype(jnp.int32)
        live = jnp.where(listed >= 0.0, 1.0, 0.0)
        counts[k : k + 1, :] = jnp.sum(live, axis=0, keepdims=True).astype(jnp.int32)
    first = pltpu.make_async_copy(cols, cols_smem, sem.at[0])
    second = pltpu.make_async_copy(counts, counts_smem, sem.at[1])
    first.start()
    second.start()
    return first, second


def build_table(base, sent_ref, turned, table):
    for row in range(24):
        turned[row] = sent_ref[:, row, :].T
    owners = 48
    segment = segments(32)
    for q in range(4):
        comps = []
        for c in range(6):
            value = None
            for k in range(4):
                part = turned[c * 4 + k, pl.ds(base, owners), :]
                if k != q:
                    part = pltpu.roll(part, (32 * (k - q)) % LANES, 1)
                value = part if value is None else jnp.where(segment == k, part, value)
            comps.append(value)
        first, second, total = [], [], None
        for c in range(3):
            c1, c2 = pieces(comps[c] * 2.0 - 1.0, 2)
            held = c1 + c2
            total = held * held if total is None else total + held * held
            first.append(-2.0 * c1)
            second.append(-2.0 * c2)
        m1, m2, m3 = pieces(total, 3)
        one, zero = jnp.ones_like(m1), jnp.zeros_like(m1)
        high, low = [], []
        for c in range(3):
            h, l = pieces(4.0 * comps[3 + c], 2)
            high.append(h)
            low.append(l)
        rows = first + [one, m1, one, m3, zero]
        rows += second + [zero, m2, zero, zero, zero]
        rows += high + low + [zero, zero]
        for f, value in enumerate(rows):
            table[pl.ds(q * 24 + f, owners, stride=96), :] = value


def evaluate_kernel(where_ref, sent_ref, order_ref, points_ref, out_ref, *scratch):
    placed, turned, table, square, weights, totals, results, cols, counts = scratch[:9]
    cols_smem, counts_smem = scratch[9:11]
    ids, sems, list_sem = scratch[11 : 11 + IDS], scratch[11 + IDS], scratch[12 + IDS]
    blocks = points_ref.shape[1] // 512
    offset = where_ref[3]
    column = where_ref[1] * 8

    def fetch(block, slot):
        source = order_ref.at[pl.ds(pl.multiple_of(block * 512, 512), 512)]
        return pltpu.make_async_copy(source, ids[slot], sems.at[slot])

    for slot in range(IDS):
        fetch(slot, slot).start()
    waits = read_lists(where_ref, sent_ref, cols, counts, cols_smem, counts_smem, list_sem)
    build_table(pl.multiple_of(offset, 16), sent_ref, turned, table)
    for wait in waits:
        wait.wait()

    def live(block):
        return counts_smem[block >> 3, column + (block & 7)]

    def chosen(block, j):
        found = cols_smem[(block >> 3) * 8 + j, column + (block & 7)] - offset * 4
        return pl.multiple_of(found * 24, 8)

    def measure(block, j):
        held = table[pl.ds(chosen(block, j), 16), :]
        centers = jnp.concatenate([held, held], 0).T.astype(BF16)
        nodes = points_ref[:, pl.ds(pl.multiple_of(block * 512, 512), 512)]
        return jnp.dot(centers, nodes, preferred_element_type=F32)

    def contract(block, j):
        held = table[pl.ds(chosen(block, j) + 16, 8), :].astype(BF16)
        coefs = jnp.concatenate([held, held], 1)
        return jnp.dot(coefs, weights[...], preferred_element_type=F32)

    def weigh(at):
        value = jnp.minimum(jnp.maximum(square[:, at], 1e-12), 1.0)
        left = 1.0 - value * lax.rsqrt(value)
        twice = left * left
        weight = (twice * twice) * (1.25 - left)
        high = weight.astype(BF16)
        weights[0:LANES, at] = high
        weights[LANES:, at] = (weight - high.astype(F32)).astype(BF16)

    def turn(slot):
        for part in range(4):
            held = totals[slot % 2, :, part * LANES : (part + 1) * LANES]
            results[slot % 2, part * LANES : (part + 1) * LANES, :] = jnp.concatenate([held] * 16, 0).T

    def place(slot, parts):
        for part in parts:
            for k in range(part * LANES, (part + 1) * LANES):
                placed[pl.ds(ids[slot][k], 1), :] = results[slot % 2, pl.ds(k, 1), :]

    def advance(slot, block, j, last, parts, ready):
        before = (slot - 1) % IDS
        if isinstance(j, int) and j == 0:
            count = live(jnp.maximum(block - 1, 0))
            added = contract(jnp.maximum(block - 1, 0), count - 1)
            held = jnp.where(count == 1, jnp.zeros_like(added), totals[before % 2])
            totals[before % 2] = held + added
        elif isinstance(j, int) and j == 1:
            totals[slot % 2] = contract(block, 0)
        else:
            totals[slot % 2] += contract(block, j - 1)
        if last is True:
            after, later = jnp.minimum(block + 1, blocks - 1), 0
        elif last is False:
            after, later = block, j + 1
        else:
            after = jnp.where(last, jnp.minimum(block + 1, blocks - 1), block)
            later = jnp.where(last, 0, j + 1)
        upcoming = measure(after, later)
        for part in range(4):
            weigh(slice(part * LANES, (part + 1) * LANES))
        square[...] = upcoming
        place((slot + 2) % IDS, parts)
        if ready:
            turn(before)

    square[...] = measure(0, 0)

    def four_blocks(step, carry):
        for slot in range(IDS):
            block = step * IDS + slot
            count = live(block)
            fetch(0, (slot + 2) % IDS).wait()

            @pl.when(count == 1)
            def _():
                advance(slot, block, 0, True, (0, 1, 2, 3), True)

            @pl.when(count == 2)
            def _():
                advance(slot, block, 0, False, (0, 1), False)
                advance(slot, block, 1, True, (2, 3), True)

            @pl.when(count == 3)
            def _():
                advance(slot, block, 0, False, (0, 1), False)
                advance(slot, block, 1, False, (2,), True)
                advance(slot, block, 2, True, (3,), False)

            @pl.when(count >= 4)
            def _():
                advance(slot, block, 0, False, (0,), False)
                advance(slot, block, 1, False, (1,), True)
                advance(slot, block, 2, False, (2,), False)
                advance(slot, block, 3, count == 4, (3,), False)

                def more(j, carry):
                    advance(slot, block, j, j + 1 == count, (), False)
                    return carry

                lax.fori_loop(4, count, more, 0)

            @pl.when(block + 2 < blocks)
            def _():
                fetch(block + 2, (slot + 2) % IDS).start()

        return carry

    lax.fori_loop(0, blocks // IDS, four_blocks, 0)

    count = live(blocks - 1)
    added = contract(blocks - 1, count - 1)
    final = (IDS - 1) % 2
    totals[final] = jnp.where(count == 1, jnp.zeros_like(added), totals[final]) + added
    turn(IDS - 1)
    for slot in (IDS - 2, IDS - 1):
        fetch(0, slot).wait()
        place(slot, (0, 1, 2, 3))
    segment = segments(8)

    def close(group, carry):
        start = pl.multiple_of(group * 2048, 2048)
        dense = placed[pl.ds(start, LANES), :]
        for g in range(1, 16):
            part = placed[pl.ds(start + g * LANES, LANES), :]
            dense = jnp.where(segment == g, part, dense)
        flat = dense.T
        for g in range(16):
            result = flat[8 * g : 8 * g + 3] + flat[8 * g + 3 : 8 * g + 6]
            out_ref[:, pl.ds(start + g * LANES, LANES)] = result
        return carry

    lax.fori_loop(0, out_ref.shape[1] // 2048, close, 0)


def evaluate_rows(where, sent, order, points):
    nodes = points.shape[1]
    vmem = pl.BlockSpec(memory_space=pltpu.VMEM)
    return pl.pallas_call(
        evaluate_kernel,
        in_specs=[
            pl.BlockSpec(memory_space=pltpu.SMEM),
            vmem,
            pl.BlockSpec(memory_space=pl.ANY),
            vmem,
        ],
        out_specs=vmem,
        out_shape=jax.ShapeDtypeStruct((3, nodes), F32),
        scratch_shapes=[
            pltpu.VMEM((nodes, LANES), F32),
            pltpu.VMEM((24, LANES, LANES), F32),
            pltpu.VMEM((192 * 24, LANES), F32),
            pltpu.VMEM((LANES, 512), F32),
            pltpu.VMEM((2 * LANES, 512), BF16),
            pltpu.VMEM((2, 8, 512), F32),
            pltpu.VMEM((2, 512, LANES), F32),
            pltpu.VMEM((LANES, LANES), jnp.int32),
            pltpu.VMEM((16, LANES), jnp.int32),
            pltpu.SMEM((LANES, LANES), jnp.int32),
            pltpu.SMEM((16, LANES), jnp.int32),
        ]
        + [pltpu.SMEM((512,), jnp.int32) for _ in range(IDS)]
        + [pltpu.SemaphoreType.DMA((IDS,)), pltpu.SemaphoreType.DMA((2,))],
        compiler_params=pltpu.CompilerParams(vmem_limit_bytes=58 * 2**20),
        cost_estimate=pl.CostEstimate(flops=10**10, bytes_accessed=100 * 2**20, transcendentals=0),
        name="evaluate_rows",
    )(where, sent, order, points)


def per_device(
    surface_pos, surface_coef, send_rows, volume_pos, relay_order, block_cols, block_count
):
    axial, azim = lax.axis_index("axial"), lax.axis_index("azim")
    slabs, sectors = lax.axis_size("axial"), lax.axis_size("azim")
    surface = jnp.concatenate([surface_pos, surface_coef], 0)
    picked = send_rows[0].reshape(-1, 4).T.reshape(-1)
    outgoing = surface.at[:, picked].get(mode="promise_in_bounds").reshape(24, -1)
    alive = jnp.arange(8, dtype=jnp.int32)[:, None] < block_count[None, :]
    listed = jnp.where(alive, block_cols.T, -1).astype(F32)
    payload = jnp.concatenate([outgoing, listed], 0)
    sent = lax.all_gather(payload, ("axial", "azim"), axis=0, tiled=False)
    order = relay_order[0]
    rows = gather_rows(order, volume_pos)
    low = jnp.clip((axial - 1) * sectors, 0, (slabs - 3) * sectors)
    where = jnp.stack([axial, azim, jnp.int32(slabs), low]).astype(jnp.int32)
    return evaluate_rows(where, sent, order, rows)


def solution(mesh):
    placed = (
        P(None, ("axial", "azim")),
        P(None, ("axial", "azim")),
        P(("axial", "azim"), None),
        P(None, ("axial", "azim")),
        P(("axial", "azim"), None),
        P(("axial", "azim"), None),
        P(("axial", "azim")),
    )
    return jax.shard_map(
        per_device,
        mesh=mesh,
        in_specs=placed,
        out_specs=P(None, ("axial", "azim")),
        check_vma=False,
    )
```

```python
import functools
import jax
import jax.numpy as jnp
from jax import lax
from jax.experimental import pallas as pl
from jax.experimental.pallas import tpu as pltpu
from jax.sharding import PartitionSpec as P

F32 = jnp.float32
BF16 = jnp.bfloat16
LANES = 128
CHUNK = 4096
SLOTS = 4
BATCH = 1024


def pieces(value, count):
    out = []
    for _ in range(count):
        part = value.astype(BF16).astype(F32)
        out.append(part)
        value = value - part
    return out


def build_rows(pos_ref, rows):
    def build(step, carry):
        start = pl.multiple_of(step * 512, 512)
        x = pos_ref[:, pl.ds(start, 512)] * 2.0 - 1.0
        x1, x2 = pieces(x, 2)
        held = x1 + x2
        n1, n2, n3 = pieces(jnp.sum(held * held, axis=0, keepdims=True), 3)
        one, zero = jnp.ones_like(n1), jnp.zeros_like(n1)
        v1 = jnp.concatenate([x1, n1, one, n3, one, zero], 0)
        v2 = jnp.concatenate([x2, n2, zero, zero, zero, zero], 0)
        stacked = jnp.concatenate(
            [v[:, g * LANES : (g + 1) * LANES] for g in range(4) for v in (v1, v1, v2, v2)], 0
        )
        dense = stacked.T
        for g in range(4):
            turned = dense if g == 0 else pltpu.roll(dense, LANES - 32 * g, 1)
            rows[pl.ds(start + g * LANES, LANES), :] = turned
        return carry

    lax.fori_loop(0, pos_ref.shape[1] // 512, build, 0, unroll=4)


def gather_kernel(order_ref, pos_ref, out_ref, rows, *rest):
    taken, ids, sems = rest[:2], rest[2 : 2 + SLOTS], rest[2 + SLOTS]
    steps = pos_ref.shape[1] // CHUNK

    def fetch(step, slot):
        start = pl.multiple_of(step * CHUNK + slot * BATCH, BATCH)
        source = order_ref.at[pl.ds(start, BATCH)]
        return pltpu.make_async_copy(source, ids[slot], sems.at[slot])

    def turn(held, start):
        for part in range(BATCH // LANES):
            flat = held[part * LANES : (part + 1) * LANES, :].T
            at = pl.ds(pl.multiple_of(start + part * LANES, LANES), LANES)
            out_ref[:, at] = flat[0:32].astype(BF16)

    for slot in range(SLOTS):
        fetch(0, slot).start()
    build_rows(pos_ref, rows)

    def one_step(step, carry):
        for slot in range(SLOTS):
            fetch(step, slot).wait()
            for k in range(BATCH):
                taken[slot % 2][pl.ds(k, 1), :] = rows[pl.ds(ids[slot][k], 1), :]
            turn(taken[1 - slot % 2], jnp.maximum(step * CHUNK + (slot - 1) * BATCH, 0))

            @pl.when(step + 1 < steps)
            def _():
                fetch(step + 1, slot).start()

        return carry

    lax.fori_loop(0, steps, one_step, 0)
    turn(taken[(SLOTS - 1) % 2], steps * CHUNK - BATCH)


def gather_rows(order, pos):
    nodes = pos.shape[1]
    vmem = pl.BlockSpec(memory_space=pltpu.VMEM)
    return pl.pallas_call(
        gather_kernel,
        in_specs=[pl.BlockSpec(memory_space=pl.ANY), vmem],
        out_specs=vmem,
        out_shape=jax.ShapeDtypeStruct((32, nodes), BF16),
        scratch_shapes=[pltpu.VMEM((nodes, LANES), F32)]
        + [pltpu.VMEM((BATCH, LANES), F32) for _ in range(2)]
        + [pltpu.SMEM((BATCH,), jnp.int32) for _ in range(SLOTS)]
        + [pltpu.SemaphoreType.DMA((SLOTS,))],
        compiler_params=pltpu.CompilerParams(vmem_limit_bytes=58 * 2**20),
        cost_estimate=pl.CostEstimate(flops=10**9, bytes_accessed=100 * 2**20, transcendentals=0),
        name="gather_rows",
    )(order, pos)


IDS = 4


def segments(width):
    return lax.broadcasted_iota(jnp.int32, (1, LANES), 1) // width


def build_table(offset, sent_ref, turned, table, cols, counts):
    owners = 48
    for row in range(12):
        turned[row] = sent_ref[:, row, :].T
    live = jnp.zeros((8, LANES), F32)
    for j in range(8):
        listed = turned[j, owners : owners + 8, :]
        cols[j * 8 : (j + 1) * 8, :] = (listed.astype(jnp.int32) - offset * 4) * 24
        live = live + jnp.where(listed >= 0.0, 1.0, 0.0)
    counts[...] = live.astype(jnp.int32)
    segment = segments(32)
    for q in range(4):
        comps = []
        for c in range(6):
            value = None
            for k in range(4):
                row = c * 4 + k
                part = turned[row % 12, 64 * (row // 12) : 64 * (row // 12) + owners, :]
                if k != q:
                    part = pltpu.roll(part, (32 * (k - q)) % LANES, 1)
                value = part if value is None else jnp.where(segment == k, part, value)
            comps.append(value)
        first, second, total = [], [], None
        for c in range(3):
            c1, c2 = pieces(comps[c] * 2.0 - 1.0, 2)
            held = c1 + c2
            total = held * held if total is None else total + held * held
            first.append(-2.0 * c1)
            second.append(-2.0 * c2)
        m1, m2, m3 = pieces(total, 3)
        one, zero = jnp.ones_like(m1), jnp.zeros_like(m1)
        high, low = [], []
        for c in range(3):
            h, l = pieces(4.0 * comps[3 + c], 2)
            high.append(h)
            low.append(l)
        rows = first + [one, m1, one, m3, zero]
        rows += second + [zero, m2, zero, zero, zero]
        rows += high + low + [zero, zero]
        for f, value in enumerate(rows):
            table[pl.ds(q * 24 + f, owners, stride=96), :] = value


def evaluate_kernel(where_ref, sent_ref, order_ref, points_ref, out_ref, *scratch):
    placed, turned, table, square, weights, centers, totals, results, cols, counts = scratch[:10]
    cols_smem, counts_smem, state = scratch[10:13]
    ids, sems, list_sem = scratch[13 : 13 + IDS], scratch[13 + IDS], scratch[14 + IDS]
    blocks = points_ref.shape[1] // 512
    column = where_ref[0] * 16

    def fetch(block, slot):
        source = order_ref.at[pl.ds(pl.multiple_of(block * 512, 512), 512)]
        return pltpu.make_async_copy(source, ids[slot], sems.at[slot])

    for slot in range(IDS):
        fetch(slot, slot).start()
    build_table(where_ref[1], sent_ref, turned, table, cols, counts)
    waits = (
        pltpu.make_async_copy(cols, cols_smem, list_sem.at[0]),
        pltpu.make_async_copy(counts, counts_smem, list_sem.at[1]),
    )
    for wait in waits:
        wait.start()
    for wait in waits:
        wait.wait()

    def live(block):
        return counts_smem[block & 7, column + (block >> 3)]

    def chosen(block, j):
        return cols_smem[j * 8 + (block & 7), column + (block >> 3)]

    def following(block, j):
        last = j + 1 >= live(block)
        after = jnp.where(last, jnp.minimum(block + 1, blocks - 1), block)
        return after, jnp.where(last, 0, j + 1)

    def bring(row):
        held = table[pl.ds(pl.multiple_of(row, 8), 16), :]
        centers[...] = jnp.concatenate([held, held], 0).T.astype(BF16)

    def measure(block):
        nodes = points_ref[:, pl.ds(pl.multiple_of(block * 512, 512), 512)]
        return jnp.dot(centers[...], nodes, preferred_element_type=F32)

    def contract(row):
        held = table[pl.ds(pl.multiple_of(row + 16, 8), 8), :].astype(BF16)
        coefs = jnp.concatenate([held, held], 1)
        held = jnp.concatenate([weights[part] for part in range(4)], 1)
        return jnp.dot(coefs, held, preferred_element_type=F32)

    def weigh(part):
        value = square[:, part * LANES : (part + 1) * LANES]
        value = jnp.minimum(jnp.maximum(value, 1e-12), 1.0)
        dist = value * lax.rsqrt(value)
        left = 1.0 - dist
        twice = left * left
        weight = (twice * twice) * (0.25 + dist)
        high = weight.astype(BF16)
        weights[part, 0:LANES, :] = high
        weights[part, LANES:, :] = (weight - high.astype(F32)).astype(BF16)

    def turn(slot):
        for part in range(4):
            held = totals[slot % 2, :, part * LANES : (part + 1) * LANES]
            results[slot % 2, part * LANES : (part + 1) * LANES, :] = jnp.concatenate([held] * 16, 0).T

    def place(slot, parts):
        for part in parts:
            for k in range(part * LANES, (part + 1) * LANES):
                placed[pl.ds(ids[slot][k], 1), :] = results[slot % 2, pl.ds(k, 1), :]

    def advance(slot, block, j, parts, ready):
        row, coming, node_block, node_j = state[1], state[2], state[3], state[4]
        added = contract(state[0])
        before = (slot - 1) % IDS
        if isinstance(j, int) and j == 0:
            alone = live(jnp.maximum(block - 1, 0)) == 1
            totals[before % 2] = jnp.where(alone, jnp.zeros_like(added), totals[before % 2]) + added
        elif isinstance(j, int) and j == 1:
            totals[slot % 2] = added
        else:
            totals[slot % 2] += added
        upcoming = measure(node_block)
        for part in range(4):
            weigh(part)
        square[...] = upcoming
        after, later = following(node_block, node_j)
        beyond = chosen(after, later)
        bring(beyond)
        state[0], state[1], state[2], state[3], state[4] = row, coming, beyond, after, later
        place((slot + 2) % IDS, parts)
        if ready:
            turn(before)

    bring(chosen(0, 0))
    square[...] = measure(0)
    after, later = following(0, 0)
    state[0], state[1], state[2] = chosen(0, 0), chosen(0, 0), chosen(after, later)
    state[3], state[4] = after, later
    bring(chosen(after, later))

    def four_blocks(step, carry):
        for slot in range(IDS):
            block = step * IDS + slot
            count = live(block)
            fetch(0, (slot + 2) % IDS).wait()

            @pl.when(count == 1)
            def _():
                advance(slot, block, 0, (0, 1, 2, 3), True)

            @pl.when(count == 2)
            def _():
                advance(slot, block, 0, (0, 1), False)
                advance(slot, block, 1, (2, 3), True)

            @pl.when(count == 3)
            def _():
                advance(slot, block, 0, (0, 1), False)
                advance(slot, block, 1, (2,), True)
                advance(slot, block, 2, (3,), False)

            @pl.when(count >= 4)
            def _():
                advance(slot, block, 0, (0,), False)
                advance(slot, block, 1, (1,), True)
                advance(slot, block, 2, (2,), False)
                advance(slot, block, 3, (3,), False)

                def more(j, carry):
                    advance(slot, block, j, (), False)
                    return carry

                lax.fori_loop(4, count, more, 0)

            @pl.when(block + 2 < blocks)
            def _():
                fetch(block + 2, (slot + 2) % IDS).start()

        return carry

    lax.fori_loop(0, blocks // IDS, four_blocks, 0)

    count = live(blocks - 1)
    added = contract(state[0])
    final = (IDS - 1) % 2
    totals[final] = jnp.where(count == 1, jnp.zeros_like(added), totals[final]) + added
    turn(IDS - 1)
    for slot in (IDS - 2, IDS - 1):
        fetch(0, slot).wait()
        place(slot, (0, 1, 2, 3))
    segment = segments(8)

    def close(group, carry):
        start = pl.multiple_of(group * 2048, 2048)
        dense = placed[pl.ds(start, LANES), :]
        for g in range(1, 16):
            part = placed[pl.ds(start + g * LANES, LANES), :]
            dense = jnp.where(segment == g, part, dense)
        flat = dense.T
        for g in range(16):
            result = flat[8 * g : 8 * g + 3] + flat[8 * g + 3 : 8 * g + 6]
            out_ref[:, pl.ds(start + g * LANES, LANES)] = result
        return carry

    lax.fori_loop(0, out_ref.shape[1] // 2048, close, 0)


def evaluate_rows(where, sent, order, points):
    nodes = points.shape[1]
    vmem = pl.BlockSpec(memory_space=pltpu.VMEM)
    return pl.pallas_call(
        evaluate_kernel,
        in_specs=[
            pl.BlockSpec(memory_space=pltpu.SMEM),
            vmem,
            pl.BlockSpec(memory_space=pl.ANY),
            vmem,
        ],
        out_specs=vmem,
        out_shape=jax.ShapeDtypeStruct((3, nodes), F32),
        scratch_shapes=[
            pltpu.VMEM((nodes, LANES), F32),
            pltpu.VMEM((12, LANES, LANES), F32),
            pltpu.VMEM((192 * 24, LANES), F32),
            pltpu.VMEM((LANES, 512), F32),
            pltpu.VMEM((4, 2 * LANES, LANES), BF16),
            pltpu.VMEM((LANES, 32), BF16),
            pltpu.VMEM((2, 8, 512), F32),
            pltpu.VMEM((2, 512, LANES), F32),
            pltpu.VMEM((64, LANES), jnp.int32),
            pltpu.VMEM((8, LANES), jnp.int32),
            pltpu.SMEM((64, LANES), jnp.int32),
            pltpu.SMEM((8, LANES), jnp.int32),
            pltpu.SMEM((8,), jnp.int32),
        ]
        + [pltpu.SMEM((512,), jnp.int32) for _ in range(IDS)]
        + [pltpu.SemaphoreType.DMA((IDS,)), pltpu.SemaphoreType.DMA((2,))],
        compiler_params=pltpu.CompilerParams(vmem_limit_bytes=58 * 2**20),
        cost_estimate=pl.CostEstimate(flops=10**10, bytes_accessed=100 * 2**20, transcendentals=0),
        name="evaluate_rows",
    )(where, sent, order, points)


def pack_kernel(outgoing_ref, cols_ref, count_ref, out_ref):
    slabs, sectors = 8, 16
    lane = lax.broadcasted_iota(jnp.int32, (1, LANES), 1)
    order = lax.broadcasted_iota(jnp.int32, (8, LANES), 0)
    listed = jnp.where(order < count_ref[...], cols_ref[...], -1).astype(F32)
    low, high = outgoing_ref[0:12], outgoing_ref[12:24]
    lists = [pltpu.roll(listed, (48 - 8 * z) % LANES, 1) for z in range(sectors)]
    for a in range(slabs):
        base = min(max((a - 1) * sectors, 0), (slabs - 3) * sectors)
        left = low if base == 0 else pltpu.roll(low, LANES - base, 1)
        right = pltpu.roll(high, (64 - base) % LANES, 1)
        rows = jnp.where(lane < 64, left, right)
        for z in range(sectors):
            out_ref[a * sectors + z, 0:8, :] = jnp.where(lane // 8 == 6, lists[z], rows[0:8])
            out_ref[a * sectors + z, 8:12, :] = rows[8:12]
            out_ref[a * sectors + z, 12:16, :] = rows[8:12]


def pack(outgoing, cols, count):
    vmem = pl.BlockSpec(memory_space=pltpu.VMEM)
    return pl.pallas_call(
        pack_kernel,
        in_specs=[vmem, vmem, vmem],
        out_specs=vmem,
        out_shape=jax.ShapeDtypeStruct((LANES, 16, LANES), F32),
        name="pack",
    )(outgoing, cols, count)


def per_device(
    surface_pos, surface_coef, send_rows, volume_pos, relay_order, block_cols, block_count
):
    axial = lax.axis_index("axial")
    slabs, sectors = lax.axis_size("axial"), lax.axis_size("azim")
    surface = jnp.concatenate([surface_pos, surface_coef], 0)
    picked = send_rows[0].reshape(-1, 4).T.reshape(-1)
    outgoing = surface.at[:, picked].get(mode="promise_in_bounds").reshape(24, -1)
    payload = pack(outgoing, block_cols.T, block_count[None])
    sent = lax.all_to_all(payload, ("axial", "azim"), split_axis=0, concat_axis=0, tiled=True)
    order = relay_order[0]
    points = gather_rows(order, volume_pos)
    low = jnp.clip((axial - 1) * sectors, 0, (slabs - 3) * sectors)
    where = jnp.stack([axial, low]).astype(jnp.int32)
    return evaluate_rows(where, sent, order, points)


def solution(mesh):
    placed = (
        P(None, ("axial", "azim")),
        P(None, ("axial", "azim")),
        P(("axial", "azim"), None),
        P(None, ("axial", "azim")),
        P(("axial", "azim"), None),
        P(("axial", "azim"), None),
        P(("axial", "azim")),
    )
    return jax.shard_map(
        per_device,
        mesh=mesh,
        in_specs=placed,
        out_specs=P(None, ("axial", "azim")),
        check_vma=False,
    )
```

```python
import functools
import jax
import jax.numpy as jnp
from jax import lax
from jax.experimental import pallas as pl
from jax.experimental.pallas import tpu as pltpu
from jax.sharding import PartitionSpec as P

F32 = jnp.float32
BF16 = jnp.bfloat16
LANES = 128
CHUNK = 4096
SLOTS = 4
BATCH = 1024


def pieces(value, count):
    out = []
    for _ in range(count):
        part = value.astype(BF16).astype(F32)
        out.append(part)
        value = value - part
    return out


def build_rows(pos_ref, rows):
    held_rows = rows.shape[0]

    def build(step, carry):
        start = pl.multiple_of(step * LANES, LANES)
        x = jnp.concatenate(
            [pos_ref[:, pl.ds(g * held_rows + start, LANES)] for g in range(4)], 1
        )
        x1, x2 = pieces(x * 2.0 - 1.0, 2)
        held = x1 + x2
        n1, n2, n3 = pieces(jnp.sum(held * held, axis=0, keepdims=True), 3)
        one, zero = jnp.ones_like(n1), jnp.zeros_like(n1)
        v1 = jnp.concatenate([x1, n1, one, n3, one, zero], 0)
        v2 = jnp.concatenate([x2, n2, zero, zero, zero, zero], 0)
        stacked = jnp.concatenate(
            [v[:, g * LANES : (g + 1) * LANES] for g in range(4) for v in (v1, v1, v2, v2)], 0
        )
        rows[pl.ds(start, LANES), :] = stacked.T
        return carry

    lax.fori_loop(0, held_rows // LANES, build, 0, unroll=4)


def gather_kernel(order_ref, source_ref, pos_ref, out_ref, rows, *rest):
    taken, ids, sems = rest[:2], rest[2 : 2 + SLOTS], rest[2 + SLOTS]
    steps = pos_ref.shape[1] // CHUNK

    def fetch(step, slot):
        start = pl.multiple_of(step * CHUNK + slot * BATCH, BATCH)
        source = source_ref.at[pl.ds(start, BATCH)]
        return pltpu.make_async_copy(source, ids[slot], sems.at[slot])

    def turn(held, start):
        for part in range(BATCH // LANES):
            flat = held[part * LANES : (part + 1) * LANES, :].T
            group = order_ref[pl.ds(start // LANES + part, 1), :] >> (rows.shape[0].bit_length() - 1)
            value = flat[0:32]
            for g in range(1, 4):
                value = jnp.where(group == g, flat[32 * g : 32 * (g + 1)], value)
            at = pl.ds(pl.multiple_of(start + part * LANES, LANES), LANES)
            out_ref[:, at] = value.astype(BF16)

    for slot in range(SLOTS):
        fetch(0, slot).start()
    build_rows(pos_ref, rows)

    def one_step(step, carry):
        for slot in range(SLOTS):
            fetch(step, slot).wait()
            for k in range(BATCH):
                taken[slot % 2][pl.ds(k, 1), :] = rows[pl.ds(ids[slot][k], 1), :]
            turn(taken[1 - slot % 2], jnp.maximum(step * CHUNK + (slot - 1) * BATCH, 0))

            @pl.when(step + 1 < steps)
            def _():
                fetch(step + 1, slot).start()

        return carry

    lax.fori_loop(0, steps, one_step, 0)
    turn(taken[(SLOTS - 1) % 2], steps * CHUNK - BATCH)


def gather_rows(order, pos):
    nodes = pos.shape[1]
    vmem = pl.BlockSpec(memory_space=pltpu.VMEM)
    return pl.pallas_call(
        gather_kernel,
        in_specs=[vmem, pl.BlockSpec(memory_space=pl.ANY), vmem],
        out_specs=vmem,
        out_shape=jax.ShapeDtypeStruct((32, nodes), BF16),
        scratch_shapes=[pltpu.VMEM((nodes // 4, LANES), F32)]
        + [pltpu.VMEM((BATCH, LANES), F32) for _ in range(2)]
        + [pltpu.SMEM((BATCH,), jnp.int32) for _ in range(SLOTS)]
        + [pltpu.SemaphoreType.DMA((SLOTS,))],
        compiler_params=pltpu.CompilerParams(vmem_limit_bytes=58 * 2**20),
        cost_estimate=pl.CostEstimate(flops=10**9, bytes_accessed=100 * 2**20, transcendentals=0),
        name="gather_rows",
    )(order.reshape(-1, LANES), order & (nodes // 4 - 1), pos)


IDS = 4


def segments(width):
    return lax.broadcasted_iota(jnp.int32, (1, LANES), 1) // width


def build_table(offset, sent_ref, turned, table, cols, counts):
    owners = 48
    for row in range(12):
        turned[row] = sent_ref[:, row, :].T
    live = jnp.zeros((8, LANES), F32)
    for j in range(8):
        listed = turned[j, owners : owners + 8, :]
        cols[j * 8 : (j + 1) * 8, :] = (listed.astype(jnp.int32) - offset * 4) * 24
        live = live + jnp.where(listed >= 0.0, 1.0, 0.0)
    counts[...] = live.astype(jnp.int32)
    segment = segments(32)
    for q in range(4):
        comps = []
        for c in range(6):
            value = None
            for k in range(4):
                row = c * 4 + k
                part = turned[row % 12, 64 * (row // 12) : 64 * (row // 12) + owners, :]
                if k != q:
                    part = pltpu.roll(part, (32 * (k - q)) % LANES, 1)
                value = part if value is None else jnp.where(segment == k, part, value)
            comps.append(value)
        first, second, total = [], [], None
        for c in range(3):
            c1, c2 = pieces(comps[c] * 2.0 - 1.0, 2)
            held = c1 + c2
            total = held * held if total is None else total + held * held
            first.append(-2.0 * c1)
            second.append(-2.0 * c2)
        m1, m2, m3 = pieces(total, 3)
        one, zero = jnp.ones_like(m1), jnp.zeros_like(m1)
        high, low = [], []
        for c in range(3):
            h, l = pieces(4.0 * comps[3 + c], 2)
            high.append(h)
            low.append(l)
        rows = first + [one, m1, one, m3, zero]
        rows += second + [zero, m2, zero, zero, zero]
        rows += high + low + [zero, zero]
        for f, value in enumerate(rows):
            table[pl.ds(q * 24 + f, owners, stride=96), :] = value


def evaluate_kernel(where_ref, sent_any, order_ref, points_any, out_ref, *scratch):
    placed, turned, table, square, weights, centers, totals, results, cols, counts = scratch[:10]
    cols_smem, counts_smem, state = scratch[10:13]
    ids, sems, list_sem = scratch[13 : 13 + IDS], scratch[13 + IDS], scratch[14 + IDS]
    sent_ref, points_ref = scratch[15 + IDS :]
    blocks = points_ref.shape[1] // 512
    column = where_ref[0] * 16

    def fetch(block, slot):
        return pltpu.make_async_copy(order_ref.at[block], ids[slot], sems.at[slot])

    for slot in range(IDS):
        fetch(slot, slot).start()
    arrive = pltpu.make_async_copy(sent_any, sent_ref, list_sem.at[2])
    arrive.start()
    follow = pltpu.make_async_copy(points_any, points_ref, list_sem.at[3])
    follow.start()
    arrive.wait()
    build_table(where_ref[1], sent_ref, turned, table, cols, counts)
    waits = (
        pltpu.make_async_copy(cols, cols_smem, list_sem.at[0]),
        pltpu.make_async_copy(counts, counts_smem, list_sem.at[1]),
    )
    for wait in waits:
        wait.start()
    for wait in waits:
        wait.wait()
    follow.wait()

    def live(block):
        return counts_smem[block & 7, column + (block >> 3)]

    def chosen(block, j):
        return cols_smem[j * 8 + (block & 7), column + (block >> 3)]

    def following(block, j):
        last = j + 1 >= live(block)
        after = jnp.where(last, jnp.minimum(block + 1, blocks - 1), block)
        return after, jnp.where(last, 0, j + 1)

    def bring(row):
        held = table[pl.ds(pl.multiple_of(row, 8), 16), :]
        centers[...] = jnp.concatenate([held, held], 0).T.astype(BF16)

    def measure(block):
        nodes = points_ref[:, pl.ds(pl.multiple_of(block * 512, 512), 512)]
        return jnp.dot(centers[...], nodes, preferred_element_type=F32)

    def contract(row):
        held = table[pl.ds(pl.multiple_of(row + 16, 8), 8), :].astype(BF16)
        coefs = jnp.concatenate([held, held], 1)
        held = jnp.concatenate([weights[part] for part in range(4)], 1)
        return jnp.dot(coefs, held, preferred_element_type=F32)

    def weigh(part):
        value = square[:, part * LANES : (part + 1) * LANES]
        value = jnp.minimum(jnp.maximum(value, 1e-12), 1.0)
        dist = value * lax.rsqrt(value)
        left = 1.0 - dist
        twice = left * left
        weight = (twice * twice) * (0.25 + dist)
        high = weight.astype(BF16)
        weights[part, 0:LANES, :] = high
        weights[part, LANES:, :] = (weight - high.astype(F32)).astype(BF16)

    def turn(slot):
        for part in range(4):
            held = totals[slot % 2, :, part * LANES : (part + 1) * LANES]
            results[slot % 2, part * LANES : (part + 1) * LANES, :] = jnp.concatenate([held] * 16, 0).T

    def place(slot, parts):
        for part in parts:
            for k in range(LANES):
                row = results[slot % 2, pl.ds(part * LANES + k, 1), :]
                placed[pl.ds(ids[slot][part, k], 1), :] = row

    def advance(slot, block, j, parts, ready):
        row, coming, node_block, node_j = state[1], state[2], state[3], state[4]
        added = contract(state[0])
        before = (slot - 1) % IDS
        if isinstance(j, int) and j == 0:
            alone = live(jnp.maximum(block - 1, 0)) == 1
            totals[before % 2] = jnp.where(alone, jnp.zeros_like(added), totals[before % 2]) + added
        elif isinstance(j, int) and j == 1:
            totals[slot % 2] = added
        else:
            totals[slot % 2] += added
        upcoming = measure(node_block)
        for part in range(4):
            weigh(part)
        square[...] = upcoming
        after, later = following(node_block, node_j)
        beyond = chosen(after, later)
        bring(beyond)
        state[0], state[1], state[2], state[3], state[4] = row, coming, beyond, after, later
        place((slot + 2) % IDS, parts)
        if ready:
            turn(before)

    bring(chosen(0, 0))
    square[...] = measure(0)
    after, later = following(0, 0)
    state[0], state[1], state[2] = chosen(0, 0), chosen(0, 0), chosen(after, later)
    state[3], state[4] = after, later
    bring(chosen(after, later))

    def four_blocks(step, carry):
        for slot in range(IDS):
            block = step * IDS + slot
            count = live(block)
            fetch(0, (slot + 2) % IDS).wait()

            @pl.when(count == 1)
            def _():
                advance(slot, block, 0, (0, 1, 2, 3), True)

            @pl.when(count == 2)
            def _():
                advance(slot, block, 0, (0, 1), False)
                advance(slot, block, 1, (2, 3), True)

            @pl.when(count == 3)
            def _():
                advance(slot, block, 0, (0, 1), False)
                advance(slot, block, 1, (2,), True)
                advance(slot, block, 2, (3,), False)

            @pl.when(count >= 4)
            def _():
                advance(slot, block, 0, (0,), False)
                advance(slot, block, 1, (1,), True)
                advance(slot, block, 2, (2,), False)
                advance(slot, block, 3, (3,), False)

                def more(j, carry):
                    advance(slot, block, j, (), False)
                    return carry

                lax.fori_loop(4, count, more, 0)

            @pl.when(block + 2 < blocks)
            def _():
                fetch(block + 2, (slot + 2) % IDS).start()

        return carry

    lax.fori_loop(0, blocks // IDS, four_blocks, 0)

    count = live(blocks - 1)
    added = contract(state[0])
    final = (IDS - 1) % 2
    totals[final] = jnp.where(count == 1, jnp.zeros_like(added), totals[final]) + added
    turn(IDS - 1)
    for slot in (IDS - 2, IDS - 1):
        fetch(0, slot).wait()
        place(slot, (0, 1, 2, 3))
    segment = segments(8)

    def close(group, carry):
        start = pl.multiple_of(group * 2048, 2048)
        dense = placed[pl.ds(start, LANES), :]
        for g in range(1, 16):
            part = placed[pl.ds(start + g * LANES, LANES), :]
            dense = jnp.where(segment == g, part, dense)
        flat = dense.T
        for g in range(16):
            result = flat[8 * g : 8 * g + 3] + flat[8 * g + 3 : 8 * g + 6]
            out_ref[:, pl.ds(start + g * LANES, LANES)] = result
        return carry

    lax.fori_loop(0, out_ref.shape[1] // 2048, close, 0)


def evaluate_rows(where, sent, order, points):
    nodes = points.shape[1]
    vmem = pl.BlockSpec(memory_space=pltpu.VMEM)
    return pl.pallas_call(
        evaluate_kernel,
        in_specs=[
            pl.BlockSpec(memory_space=pltpu.SMEM),
            pl.BlockSpec(memory_space=pl.ANY),
            vmem,
            pl.BlockSpec(memory_space=pl.ANY),
        ],
        out_specs=vmem,
        out_shape=jax.ShapeDtypeStruct((3, nodes), F32),
        scratch_shapes=[
            pltpu.VMEM((nodes, LANES), F32),
            pltpu.VMEM((12, LANES, LANES), F32),
            pltpu.VMEM((192 * 24, LANES), F32),
            pltpu.VMEM((LANES, 512), F32),
            pltpu.VMEM((4, 2 * LANES, LANES), BF16),
            pltpu.VMEM((LANES, 32), BF16),
            pltpu.VMEM((2, 8, 512), F32),
            pltpu.VMEM((2, 512, LANES), F32),
            pltpu.VMEM((64, LANES), jnp.int32),
            pltpu.VMEM((8, LANES), jnp.int32),
            pltpu.SMEM((64, LANES), jnp.int32),
            pltpu.SMEM((8, LANES), jnp.int32),
            pltpu.SMEM((8,), jnp.int32),
        ]
        + [pltpu.SMEM((4, LANES), jnp.int32) for _ in range(IDS)]
        + [pltpu.SemaphoreType.DMA((IDS,)), pltpu.SemaphoreType.DMA((4,))]
        + [pltpu.VMEM(sent.shape, F32), pltpu.VMEM(points.shape, BF16)],
        compiler_params=pltpu.CompilerParams(vmem_limit_bytes=58 * 2**20),
        cost_estimate=pl.CostEstimate(flops=10**10, bytes_accessed=100 * 2**20, transcendentals=0),
        name="evaluate_rows",
    )(where, sent, order.reshape(-1, 4, LANES), points)


def pack_kernel(outgoing_ref, cols_ref, count_ref, out_ref):
    slabs, sectors = 8, 16
    lane = lax.broadcasted_iota(jnp.int32, (1, LANES), 1)
    order = lax.broadcasted_iota(jnp.int32, (8, LANES), 0)
    listed = jnp.where(order < count_ref[...], cols_ref[...], -1).astype(F32)
    low, high = outgoing_ref[0:12], outgoing_ref[12:24]
    lists = [pltpu.roll(listed, (48 - 8 * z) % LANES, 1) for z in range(sectors)]
    for a in range(slabs):
        base = min(max((a - 1) * sectors, 0), (slabs - 3) * sectors)
        left = low if base == 0 else pltpu.roll(low, LANES - base, 1)
        right = pltpu.roll(high, (64 - base) % LANES, 1)
        rows = jnp.where(lane < 64, left, right)
        for z in range(sectors):
            out_ref[a * sectors + z, 0:8, :] = jnp.where(lane // 8 == 6, lists[z], rows[0:8])
            out_ref[a * sectors + z, 8:12, :] = rows[8:12]
            out_ref[a * sectors + z, 12:16, :] = rows[8:12]


def pack(outgoing, cols, count):
    vmem = pl.BlockSpec(memory_space=pltpu.VMEM)
    return pl.pallas_call(
        pack_kernel,
        in_specs=[vmem, vmem, vmem],
        out_specs=vmem,
        out_shape=jax.ShapeDtypeStruct((LANES, 16, LANES), F32),
        name="pack",
    )(outgoing, cols, count)


def per_device(
    surface_pos, surface_coef, send_rows, volume_pos, relay_order, block_cols, block_count
):
    axial = lax.axis_index("axial")
    slabs, sectors = lax.axis_size("axial"), lax.axis_size("azim")
    surface = jnp.concatenate([surface_pos, surface_coef], 0)
    picked = send_rows[0].reshape(-1, 4).T.reshape(-1)
    outgoing = surface.at[:, picked].get(mode="promise_in_bounds").reshape(24, -1)
    payload = pack(outgoing, block_cols.T, block_count[None])
    sent = lax.all_to_all(payload, ("axial", "azim"), split_axis=0, concat_axis=0, tiled=True)
    order = relay_order[0]
    points = gather_rows(order, volume_pos)
    low = jnp.clip((axial - 1) * sectors, 0, (slabs - 3) * sectors)
    where = jnp.stack([axial, low]).astype(jnp.int32)
    return evaluate_rows(where, sent, order, points)


def solution(mesh):
    placed = (
        P(None, ("axial", "azim")),
        P(None, ("axial", "azim")),
        P(("axial", "azim"), None),
        P(None, ("axial", "azim")),
        P(("axial", "azim"), None),
        P(("axial", "azim"), None),
        P(("axial", "azim")),
    )
    return jax.shard_map(
        per_device,
        mesh=mesh,
        in_specs=placed,
        out_specs=P(None, ("axial", "azim")),
        check_vma=False,
    )
```

```python
import functools
import jax
import jax.numpy as jnp
from jax import lax
from jax.experimental import pallas as pl
from jax.experimental.pallas import tpu as pltpu
from jax.sharding import PartitionSpec as P

F32 = jnp.float32
BF16 = jnp.bfloat16
LANES = 128
CHUNK = 4096
SLOTS = 4
BATCH = 1024


def pieces(value, count):
    out = []
    for _ in range(count):
        part = value.astype(BF16).astype(F32)
        out.append(part)
        value = value - part
    return out


def build_rows(pos_ref, rows):
    held_rows = rows.shape[0]

    def build(step, carry):
        start = pl.multiple_of(step * LANES, LANES)
        x = jnp.concatenate(
            [pos_ref[:, pl.ds(g * held_rows + start, LANES)] for g in range(4)], 1
        )
        x1, x2 = pieces(x * 2.0 - 1.0, 2)
        held = x1 + x2
        n1, n2, n3 = pieces(jnp.sum(held * held, axis=0, keepdims=True), 3)
        one, zero = jnp.ones_like(n1), jnp.zeros_like(n1)
        v1 = jnp.concatenate([x1, n1, one, n3, one, zero], 0)
        v2 = jnp.concatenate([x2, n2, zero, zero, zero, zero], 0)
        stacked = jnp.concatenate(
            [v[:, g * LANES : (g + 1) * LANES] for g in range(4) for v in (v1, v1, v2, v2)], 0
        )
        rows[pl.ds(start, LANES), :] = stacked.T
        return carry

    lax.fori_loop(0, held_rows // LANES, build, 0, unroll=4)


def gather_kernel(order_ref, source_ref, pos_ref, out_ref, rows, *rest):
    taken, ids, sems = rest[:2], rest[2 : 2 + SLOTS], rest[2 + SLOTS]
    steps = pos_ref.shape[1] // CHUNK

    def fetch(step, slot):
        start = pl.multiple_of(step * CHUNK + slot * BATCH, BATCH)
        source = source_ref.at[pl.ds(start, BATCH)]
        return pltpu.make_async_copy(source, ids[slot], sems.at[slot])

    def turn(held, start):
        for part in range(BATCH // LANES):
            flat = held[part * LANES : (part + 1) * LANES, :].T
            group = order_ref[pl.ds(start // LANES + part, 1), :] >> (rows.shape[0].bit_length() - 1)
            value = flat[0:32]
            for g in range(1, 4):
                value = jnp.where(group == g, flat[32 * g : 32 * (g + 1)], value)
            at = pl.ds(pl.multiple_of(start + part * LANES, LANES), LANES)
            out_ref[:, at] = value.astype(BF16)

    for slot in range(SLOTS):
        fetch(0, slot).start()
    build_rows(pos_ref, rows)

    def one_step(step, carry):
        for slot in range(SLOTS):
            fetch(step, slot).wait()
            for k in range(BATCH):
                taken[slot % 2][pl.ds(k, 1), :] = rows[pl.ds(ids[slot][k], 1), :]
            turn(taken[1 - slot % 2], jnp.maximum(step * CHUNK + (slot - 1) * BATCH, 0))

            @pl.when(step + 1 < steps)
            def _():
                fetch(step + 1, slot).start()

        return carry

    lax.fori_loop(0, steps, one_step, 0)
    turn(taken[(SLOTS - 1) % 2], steps * CHUNK - BATCH)


def gather_rows(order, pos):
    nodes = pos.shape[1]
    vmem = pl.BlockSpec(memory_space=pltpu.VMEM)
    return pl.pallas_call(
        gather_kernel,
        in_specs=[vmem, pl.BlockSpec(memory_space=pl.ANY), vmem],
        out_specs=vmem,
        out_shape=jax.ShapeDtypeStruct((32, nodes), BF16),
        scratch_shapes=[pltpu.VMEM((nodes // 4, LANES), F32)]
        + [pltpu.VMEM((BATCH, LANES), F32) for _ in range(2)]
        + [pltpu.SMEM((BATCH,), jnp.int32) for _ in range(SLOTS)]
        + [pltpu.SemaphoreType.DMA((SLOTS,))],
        compiler_params=pltpu.CompilerParams(vmem_limit_bytes=58 * 2**20),
        cost_estimate=pl.CostEstimate(flops=10**9, bytes_accessed=100 * 2**20, transcendentals=0),
        name="gather_rows",
    )(order.reshape(-1, LANES), order & (nodes // 4 - 1), pos)


IDS = 4


def segments(width):
    return lax.broadcasted_iota(jnp.int32, (1, LANES), 1) // width


def build_table(offset, sent_ref, turned, table, cols, counts):
    owners = 48
    for row in range(12):
        turned[row] = sent_ref[:, row, :].T
    live = jnp.zeros((8, LANES), F32)
    for j in range(8):
        listed = turned[j, owners : owners + 8, :]
        cols[j * 8 : (j + 1) * 8, :] = (listed.astype(jnp.int32) - offset * 4) * 24
        live = live + jnp.where(listed >= 0.0, 1.0, 0.0)
    counts[...] = live.astype(jnp.int32)
    segment = segments(32)
    for q in range(4):
        comps = []
        for c in range(6):
            value = None
            for k in range(4):
                row = c * 4 + k
                part = turned[row % 12, 64 * (row // 12) : 64 * (row // 12) + owners, :]
                if k != q:
                    part = pltpu.roll(part, (32 * (k - q)) % LANES, 1)
                value = part if value is None else jnp.where(segment == k, part, value)
            comps.append(value)
        first, second, total = [], [], None
        for c in range(3):
            c1, c2 = pieces(comps[c] * 2.0 - 1.0, 2)
            held = c1 + c2
            total = held * held if total is None else total + held * held
            first.append(-2.0 * c1)
            second.append(-2.0 * c2)
        m1, m2, m3 = pieces(total, 3)
        one, zero = jnp.ones_like(m1), jnp.zeros_like(m1)
        high, low = [], []
        for c in range(3):
            h, l = pieces(4.0 * comps[3 + c], 2)
            high.append(h)
            low.append(l)
        rows = first + [one, m1, one, m3, zero]
        rows += second + [zero, m2, zero, zero, zero]
        rows += high + low + [zero, zero]
        for f, value in enumerate(rows):
            table[pl.ds(q * 24 + f, owners, stride=96), :] = value


def evaluate_kernel(where_ref, sent_any, order_ref, points_any, out_ref, *scratch):
    placed, turned, table, square, weights, centers, totals, results, cols, counts = scratch[:10]
    cols_smem, counts_smem, state = scratch[10:13]
    ids, sems, list_sem = scratch[13 : 13 + IDS], scratch[13 + IDS], scratch[14 + IDS]
    sent_ref, points_ref = scratch[15 + IDS :]
    blocks = points_ref.shape[1] // 512
    column = where_ref[0] * 16

    def fetch(block, slot):
        return pltpu.make_async_copy(order_ref.at[block], ids[slot], sems.at[slot])

    for slot in range(IDS):
        fetch(slot, slot).start()
    arrive = pltpu.make_async_copy(sent_any, sent_ref, list_sem.at[2])
    arrive.start()
    follow = pltpu.make_async_copy(points_any, points_ref, list_sem.at[3])
    follow.start()
    arrive.wait()
    build_table(where_ref[1], sent_ref, turned, table, cols, counts)
    waits = (
        pltpu.make_async_copy(cols, cols_smem, list_sem.at[0]),
        pltpu.make_async_copy(counts, counts_smem, list_sem.at[1]),
    )
    for wait in waits:
        wait.start()
    for wait in waits:
        wait.wait()
    follow.wait()

    def live(block):
        return counts_smem[block & 7, column + (block >> 3)]

    def chosen(block, j):
        return cols_smem[j * 8 + (block & 7), column + (block >> 3)]

    def following(block, j):
        last = j + 1 >= live(block)
        after = jnp.where(last, jnp.minimum(block + 1, blocks - 1), block)
        return after, jnp.where(last, 0, j + 1)

    def bring(row):
        held = table[pl.ds(pl.multiple_of(row, 8), 16), :]
        centers[...] = jnp.concatenate([held, held], 0).T.astype(BF16)

    def measure(block):
        nodes = points_ref[:, pl.ds(pl.multiple_of(block * 512, 512), 512)]
        return jnp.dot(centers[...], nodes, preferred_element_type=F32)

    def contract(row):
        held = table[pl.ds(pl.multiple_of(row + 16, 8), 8), :].astype(BF16)
        coefs = jnp.concatenate([held, held], 1)
        held = jnp.concatenate([weights[part] for part in range(4)], 1)
        return jnp.dot(coefs, held, preferred_element_type=F32)

    def weigh(part):
        value = square[:, part * LANES : (part + 1) * LANES]
        value = jnp.minimum(jnp.maximum(value, 1e-12), 1.0)
        dist = value * lax.rsqrt(value)
        left = 1.0 - dist
        twice = left * left
        weight = (twice * twice) * (0.25 + dist)
        high = weight.astype(BF16)
        weights[part, 0:LANES, :] = high
        weights[part, LANES:, :] = (weight - high.astype(F32)).astype(BF16)

    def turn(slot):
        for part in range(4):
            held = totals[slot % 2, :, part * LANES : (part + 1) * LANES]
            results[slot % 2, part * LANES : (part + 1) * LANES, :] = jnp.concatenate([held] * 16, 0).T

    def place(slot, parts):
        for part in parts:
            for k in range(LANES):
                row = results[slot % 2, pl.ds(part * LANES + k, 1), :]
                placed[pl.ds(ids[slot][part, k], 1), :] = row

    def advance(slot, block, j, parts, ready):
        row, coming, node_block, node_j = state[1], state[2], state[3], state[4]
        added = contract(state[0])
        before = (slot - 1) % IDS
        if isinstance(j, int) and j == 0:
            alone = live(jnp.maximum(block - 1, 0)) == 1
            totals[before % 2] = jnp.where(alone, jnp.zeros_like(added), totals[before % 2]) + added
        elif isinstance(j, int) and j == 1:
            totals[slot % 2] = added
        else:
            totals[slot % 2] += added
        upcoming = measure(node_block)
        for part in range(4):
            weigh(part)
        square[...] = upcoming
        after, later = following(node_block, node_j)
        beyond = chosen(after, later)
        bring(beyond)
        state[0], state[1], state[2], state[3], state[4] = row, coming, beyond, after, later
        place((slot + 2) % IDS, parts)
        if ready:
            turn(before)

    bring(chosen(0, 0))
    square[...] = measure(0)
    after, later = following(0, 0)
    state[0], state[1], state[2] = chosen(0, 0), chosen(0, 0), chosen(after, later)
    state[3], state[4] = after, later
    bring(chosen(after, later))

    def four_blocks(step, carry):
        for slot in range(IDS):
            block = step * IDS + slot
            count = live(block)
            fetch(0, (slot + 2) % IDS).wait()

            @pl.when(count == 1)
            def _():
                advance(slot, block, 0, (0, 1, 2, 3), True)

            @pl.when(count == 2)
            def _():
                advance(slot, block, 0, (0, 1), False)
                advance(slot, block, 1, (2, 3), True)

            @pl.when(count == 3)
            def _():
                advance(slot, block, 0, (0, 1), False)
                advance(slot, block, 1, (2,), True)
                advance(slot, block, 2, (3,), False)

            @pl.when(count >= 4)
            def _():
                advance(slot, block, 0, (0,), False)
                advance(slot, block, 1, (1,), True)
                advance(slot, block, 2, (2,), False)
                advance(slot, block, 3, (3,), False)

                def more(j, carry):
                    advance(slot, block, j, (), False)
                    return carry

                lax.fori_loop(4, count, more, 0)

            @pl.when(block + 2 < blocks)
            def _():
                fetch(block + 2, (slot + 2) % IDS).start()

        return carry

    lax.fori_loop(0, blocks // IDS, four_blocks, 0)

    count = live(blocks - 1)
    added = contract(state[0])
    final = (IDS - 1) % 2
    totals[final] = jnp.where(count == 1, jnp.zeros_like(added), totals[final]) + added
    turn(IDS - 1)
    for slot in (IDS - 2, IDS - 1):
        fetch(0, slot).wait()
        place(slot, (0, 1, 2, 3))
    segment = segments(8)

    def close(group, carry):
        start = pl.multiple_of(group * 2048, 2048)
        dense = placed[pl.ds(start, LANES), :]
        for g in range(1, 16):
            part = placed[pl.ds(start + g * LANES, LANES), :]
            dense = jnp.where(segment == g, part, dense)
        flat = dense.T
        for g in range(16):
            result = flat[8 * g : 8 * g + 3] + flat[8 * g + 3 : 8 * g + 6]
            out_ref[:, pl.ds(start + g * LANES, LANES)] = result
        return carry

    lax.fori_loop(0, out_ref.shape[1] // 2048, close, 0)


def evaluate_rows(where, sent, order, points):
    nodes = points.shape[1]
    vmem = pl.BlockSpec(memory_space=pltpu.VMEM)
    return pl.pallas_call(
        evaluate_kernel,
        in_specs=[
            pl.BlockSpec(memory_space=pltpu.SMEM),
            pl.BlockSpec(memory_space=pl.ANY),
            vmem,
            pl.BlockSpec(memory_space=pl.ANY),
        ],
        out_specs=vmem,
        out_shape=jax.ShapeDtypeStruct((3, nodes), F32),
        scratch_shapes=[
            pltpu.VMEM((nodes, LANES), F32),
            pltpu.VMEM((12, LANES, LANES), F32),
            pltpu.VMEM((192 * 24, LANES), F32),
            pltpu.VMEM((LANES, 512), F32),
            pltpu.VMEM((4, 2 * LANES, LANES), BF16),
            pltpu.VMEM((LANES, 32), BF16),
            pltpu.VMEM((2, 8, 512), F32),
            pltpu.VMEM((2, 512, LANES), F32),
            pltpu.VMEM((64, LANES), jnp.int32),
            pltpu.VMEM((8, LANES), jnp.int32),
            pltpu.SMEM((64, LANES), jnp.int32),
            pltpu.SMEM((8, LANES), jnp.int32),
            pltpu.SMEM((8,), jnp.int32),
        ]
        + [pltpu.SMEM((4, LANES), jnp.int32) for _ in range(IDS)]
        + [pltpu.SemaphoreType.DMA((IDS,)), pltpu.SemaphoreType.DMA((4,))]
        + [pltpu.VMEM(sent.shape, F32), pltpu.VMEM(points.shape, BF16)],
        compiler_params=pltpu.CompilerParams(vmem_limit_bytes=58 * 2**20),
        cost_estimate=pl.CostEstimate(flops=10**10, bytes_accessed=100 * 2**20, transcendentals=0),
        name="evaluate_rows",
    )(where, sent, order.reshape(-1, 4, LANES), points)


def pick(source, index):
    return jnp.take_along_axis(source, index, axis=1, mode="promise_in_bounds")


def pack_kernel(pos_ref, coef_ref, send_ref, cols_ref, count_ref, out_ref):
    slabs, sectors = 8, 16
    lane = lax.broadcasted_iota(jnp.int32, (1, LANES), 1)
    order = lax.broadcasted_iota(jnp.int32, (8, LANES), 0)
    surface = jnp.concatenate([pos_ref[...], coef_ref[...], coef_ref[0:2]], 0)
    wanted = 4 * lax.broadcasted_iota(jnp.int32, (8, LANES), 1) + (order & 3)
    sent = None
    for part in range(4):
        held = jnp.broadcast_to(send_ref[:, part * LANES : (part + 1) * LANES], (8, LANES))
        found = pick(held, wanted & (LANES - 1))
        sent = found if sent is None else jnp.where(wanted >> 7 == part, found, sent)
    picked = []
    for k in range(4):
        node = jnp.broadcast_to(sent[k : k + 1], (8, LANES))
        value = None
        for part in range(8):
            found = pick(surface[:, part * LANES : (part + 1) * LANES], node & (LANES - 1))
            value = found if value is None else jnp.where(node >> 7 == part, found, value)
        picked.append(value)
    low = jnp.concatenate([picked[k][c : c + 1] for c in range(3) for k in range(4)], 0)
    high = jnp.concatenate([picked[k][c : c + 1] for c in range(3, 6) for k in range(4)], 0)
    listed = jnp.where(order < count_ref[...], cols_ref[...], -1).astype(F32)
    lists = [pltpu.roll(listed, (48 - 8 * z) % LANES, 1) for z in range(sectors)]
    for a in range(slabs):
        base = min(max((a - 1) * sectors, 0), (slabs - 3) * sectors)
        left = low if base == 0 else pltpu.roll(low, LANES - base, 1)
        right = pltpu.roll(high, (64 - base) % LANES, 1)
        rows = jnp.where(lane < 64, left, right)
        for z in range(sectors):
            out_ref[a * sectors + z, 0:8, :] = jnp.where(lane // 8 == 6, lists[z], rows[0:8])
            out_ref[a * sectors + z, 8:12, :] = rows[8:12]
            out_ref[a * sectors + z, 12:16, :] = rows[8:12]


def pack(*operands):
    vmem = pl.BlockSpec(memory_space=pltpu.VMEM)
    return pl.pallas_call(
        pack_kernel,
        in_specs=[vmem] * 5,
        out_specs=vmem,
        out_shape=jax.ShapeDtypeStruct((LANES, 16, LANES), F32),
        name="pack",
    )(*operands)


def per_device(
    surface_pos, surface_coef, send_rows, volume_pos, relay_order, block_cols, block_count
):
    axial = lax.axis_index("axial")
    slabs, sectors = lax.axis_size("axial"), lax.axis_size("azim")
    payload = pack(surface_pos, surface_coef, send_rows, block_cols.T, block_count[None])
    sent = lax.all_to_all(payload, ("axial", "azim"), split_axis=0, concat_axis=0, tiled=True)
    order = relay_order[0]
    points = gather_rows(order, volume_pos)
    low = jnp.clip((axial - 1) * sectors, 0, (slabs - 3) * sectors)
    where = jnp.stack([axial, low]).astype(jnp.int32)
    return evaluate_rows(where, sent, order, points)


def solution(mesh):
    placed = (
        P(None, ("axial", "azim")),
        P(None, ("axial", "azim")),
        P(("axial", "azim"), None),
        P(None, ("axial", "azim")),
        P(("axial", "azim"), None),
        P(("axial", "azim"), None),
        P(("axial", "azim")),
    )
    return jax.shard_map(
        per_device,
        mesh=mesh,
        in_specs=placed,
        out_specs=P(None, ("axial", "azim")),
        check_vma=False,
    )
```

```python
import functools
import jax
import jax.numpy as jnp
from jax import lax
from jax.experimental import pallas as pl
from jax.experimental.pallas import tpu as pltpu
from jax.sharding import PartitionSpec as P

F32 = jnp.float32
BF16 = jnp.bfloat16
LANES = 128
CHUNK = 4096
SLOTS = 4
BATCH = 1024


def pieces(value, count):
    out = []
    for _ in range(count):
        part = value.astype(BF16).astype(F32)
        out.append(part)
        value = value - part
    return out


def build_rows(pos_ref, rows):
    held_rows = rows.shape[0]

    def build(step, carry):
        start = pl.multiple_of(step * LANES, LANES)
        x = jnp.concatenate(
            [pos_ref[:, pl.ds(g * held_rows + start, LANES)] for g in range(4)], 1
        )
        x1, x2 = pieces(x * 2.0 - 1.0, 2)
        held = x1 + x2
        n1, n2, n3 = pieces(jnp.sum(held * held, axis=0, keepdims=True), 3)
        one, zero = jnp.ones_like(n1), jnp.zeros_like(n1)
        v1 = jnp.concatenate([x1, n1, one, n3, one, zero], 0)
        v2 = jnp.concatenate([x2, n2, zero, zero, zero, zero], 0)
        stacked = jnp.concatenate(
            [v[:, g * LANES : (g + 1) * LANES] for g in range(4) for v in (v1, v1, v2, v2)], 0
        )
        rows[pl.ds(start, LANES), :] = stacked.T
        return carry

    lax.fori_loop(0, held_rows // LANES, build, 0, unroll=4)


def gather_kernel(order_ref, pos_ref, out_ref, rows, source_ref, *rest):
    taken, ids, sems = rest[:2], rest[2 : 2 + SLOTS], rest[2 + SLOTS]
    steps = pos_ref.shape[1] // CHUNK

    def fetch(step, slot):
        start = pl.multiple_of((step * CHUNK + slot * BATCH) // LANES, BATCH // LANES)
        source = source_ref.at[pl.ds(start, BATCH // LANES)]
        return pltpu.make_async_copy(source, ids[slot], sems.at[slot])

    def turn(held, start):
        for part in range(BATCH // LANES):
            flat = held[part * LANES : (part + 1) * LANES, :].T
            group = order_ref[pl.ds(start // LANES + part, 1), :] >> (rows.shape[0].bit_length() - 1)
            value = flat[0:32]
            for g in range(1, 4):
                value = jnp.where(group == g, flat[32 * g : 32 * (g + 1)], value)
            at = pl.ds(pl.multiple_of(start + part * LANES, LANES), LANES)
            out_ref[:, at] = value.astype(BF16)

    source_ref[...] = order_ref[...] & (rows.shape[0] - 1)
    for slot in range(SLOTS):
        fetch(0, slot).start()
    build_rows(pos_ref, rows)

    def one_step(step, carry):
        for slot in range(SLOTS):
            fetch(step, slot).wait()
            for k in range(BATCH):
                taken[slot % 2][pl.ds(k, 1), :] = rows[pl.ds(ids[slot][k // LANES, k % LANES], 1), :]
            turn(taken[1 - slot % 2], jnp.maximum(step * CHUNK + (slot - 1) * BATCH, 0))

            @pl.when(step + 1 < steps)
            def _():
                fetch(step + 1, slot).start()

        return carry

    lax.fori_loop(0, steps, one_step, 0)
    turn(taken[(SLOTS - 1) % 2], steps * CHUNK - BATCH)


def gather_rows(order, pos):
    nodes = pos.shape[1]
    vmem = pl.BlockSpec(memory_space=pltpu.VMEM)
    return pl.pallas_call(
        gather_kernel,
        in_specs=[vmem, vmem],
        out_specs=vmem,
        out_shape=jax.ShapeDtypeStruct((32, nodes), BF16),
        scratch_shapes=[pltpu.VMEM((nodes // 4, LANES), F32), pltpu.VMEM((nodes // LANES, LANES), jnp.int32)]
        + [pltpu.VMEM((BATCH, LANES), F32) for _ in range(2)]
        + [pltpu.SMEM((BATCH // LANES, LANES), jnp.int32) for _ in range(SLOTS)]
        + [pltpu.SemaphoreType.DMA((SLOTS,))],
        compiler_params=pltpu.CompilerParams(vmem_limit_bytes=58 * 2**20),
        cost_estimate=pl.CostEstimate(flops=10**9, bytes_accessed=100 * 2**20, transcendentals=0),
        name="gather_rows",
    )(order.reshape(-1, LANES), pos)


IDS = 4


def segments(width):
    return lax.broadcasted_iota(jnp.int32, (1, LANES), 1) // width


def build_table(offset, sent_ref, turned, table, cols, counts):
    owners = 48
    for row in range(12):
        turned[row] = sent_ref[:, row, :].T
    live = jnp.zeros((8, LANES), F32)
    for j in range(8):
        listed = turned[j, owners : owners + 8, :]
        cols[j * 8 : (j + 1) * 8, :] = (listed.astype(jnp.int32) - offset * 4) * 24
        live = live + jnp.where(listed >= 0.0, 1.0, 0.0)
    counts[...] = live.astype(jnp.int32)
    segment = segments(32)
    for q in range(4):
        comps = []
        for c in range(6):
            value = None
            for k in range(4):
                row = c * 4 + k
                part = turned[row % 12, 64 * (row // 12) : 64 * (row // 12) + owners, :]
                if k != q:
                    part = pltpu.roll(part, (32 * (k - q)) % LANES, 1)
                value = part if value is None else jnp.where(segment == k, part, value)
            comps.append(value)
        first, second, total = [], [], None
        for c in range(3):
            c1, c2 = pieces(comps[c] * 2.0 - 1.0, 2)
            held = c1 + c2
            total = held * held if total is None else total + held * held
            first.append(-2.0 * c1)
            second.append(-2.0 * c2)
        m1, m2, m3 = pieces(total, 3)
        one, zero = jnp.ones_like(m1), jnp.zeros_like(m1)
        high, low = [], []
        for c in range(3):
            h, l = pieces(4.0 * comps[3 + c], 2)
            high.append(h)
            low.append(l)
        rows = first + [one, m1, one, m3, zero]
        rows += second + [zero, m2, zero, zero, zero]
        rows += high + low + [zero, zero]
        for f, value in enumerate(rows):
            table[pl.ds(q * 24 + f, owners, stride=96), :] = value


def evaluate_kernel(sent_any, order_ref, points_any, out_ref, *scratch):
    placed, turned, table, square, weights, centers, totals, results, cols, counts = scratch[:10]
    cols_smem, counts_smem, state = scratch[10:13]
    ids, sems, list_sem = scratch[13 : 13 + IDS], scratch[13 + IDS], scratch[14 + IDS]
    sent_ref, points_ref = scratch[15 + IDS :]
    blocks = points_ref.shape[1] // 512
    axial = lax.axis_index("axial")
    column = axial * 16
    low = jnp.clip((axial - 1) * 16, 0, (lax.axis_size("axial") - 3) * 16)

    def fetch(block, slot):
        return pltpu.make_async_copy(order_ref.at[block], ids[slot], sems.at[slot])

    for slot in range(IDS):
        fetch(slot, slot).start()
    arrive = pltpu.make_async_copy(sent_any, sent_ref, list_sem.at[2])
    arrive.start()
    follow = pltpu.make_async_copy(points_any, points_ref, list_sem.at[3])
    follow.start()
    arrive.wait()
    build_table(low, sent_ref, turned, table, cols, counts)
    waits = (
        pltpu.make_async_copy(cols, cols_smem, list_sem.at[0]),
        pltpu.make_async_copy(counts, counts_smem, list_sem.at[1]),
    )
    for wait in waits:
        wait.start()
    for wait in waits:
        wait.wait()
    follow.wait()

    def live(block):
        return counts_smem[block & 7, column + (block >> 3)]

    def chosen(block, j):
        return cols_smem[j * 8 + (block & 7), column + (block >> 3)]

    def following(block, j):
        last = j + 1 >= live(block)
        after = jnp.where(last, jnp.minimum(block + 1, blocks - 1), block)
        return after, jnp.where(last, 0, j + 1)

    def bring(row):
        held = table[pl.ds(pl.multiple_of(row, 8), 16), :]
        centers[...] = jnp.concatenate([held, held], 0).T.astype(BF16)

    def measure(block):
        nodes = points_ref[:, pl.ds(pl.multiple_of(block * 512, 512), 512)]
        return jnp.dot(centers[...], nodes, preferred_element_type=F32)

    def contract(row):
        held = table[pl.ds(pl.multiple_of(row + 16, 8), 8), :].astype(BF16)
        coefs = jnp.concatenate([held, held], 1)
        held = jnp.concatenate([weights[part] for part in range(4)], 1)
        return jnp.dot(coefs, held, preferred_element_type=F32)

    def weigh(part):
        value = square[:, part * LANES : (part + 1) * LANES]
        value = jnp.minimum(jnp.maximum(value, 1e-12), 1.0)
        dist = value * lax.rsqrt(value)
        left = 1.0 - dist
        twice = left * left
        weight = (twice * twice) * (0.25 + dist)
        high = weight.astype(BF16)
        weights[part, 0:LANES, :] = high
        weights[part, LANES:, :] = (weight - high.astype(F32)).astype(BF16)

    def turn(slot):
        for part in range(4):
            held = totals[slot % 2, :, part * LANES : (part + 1) * LANES]
            results[slot % 2, part * LANES : (part + 1) * LANES, :] = jnp.concatenate([held] * 16, 0).T

    def place(slot, parts):
        for part in parts:
            for k in range(LANES):
                row = results[slot % 2, pl.ds(part * LANES + k, 1), :]
                placed[pl.ds(ids[slot][part, k], 1), :] = row

    def advance(slot, block, j, parts, ready):
        row, coming, node_block, node_j = state[1], state[2], state[3], state[4]
        added = contract(state[0])
        before = (slot - 1) % IDS
        if isinstance(j, int) and j == 0:
            alone = live(jnp.maximum(block - 1, 0)) == 1
            totals[before % 2] = jnp.where(alone, jnp.zeros_like(added), totals[before % 2]) + added
        elif isinstance(j, int) and j == 1:
            totals[slot % 2] = added
        else:
            totals[slot % 2] += added
        upcoming = measure(node_block)
        for part in range(4):
            weigh(part)
        square[...] = upcoming
        after, later = following(node_block, node_j)
        beyond = chosen(after, later)
        bring(beyond)
        state[0], state[1], state[2], state[3], state[4] = row, coming, beyond, after, later
        place((slot + 2) % IDS, parts)
        if ready:
            turn(before)

    bring(chosen(0, 0))
    square[...] = measure(0)
    after, later = following(0, 0)
    state[0], state[1], state[2] = chosen(0, 0), chosen(0, 0), chosen(after, later)
    state[3], state[4] = after, later
    bring(chosen(after, later))

    def four_blocks(step, carry):
        for slot in range(IDS):
            block = step * IDS + slot
            count = live(block)
            fetch(0, (slot + 2) % IDS).wait()

            @pl.when(count == 1)
            def _():
                advance(slot, block, 0, (0, 1, 2, 3), True)

            @pl.when(count == 2)
            def _():
                advance(slot, block, 0, (0, 1), False)
                advance(slot, block, 1, (2, 3), True)

            @pl.when(count == 3)
            def _():
                advance(slot, block, 0, (0, 1), False)
                advance(slot, block, 1, (2,), True)
                advance(slot, block, 2, (3,), False)

            @pl.when(count >= 4)
            def _():
                advance(slot, block, 0, (0,), False)
                advance(slot, block, 1, (1,), True)
                advance(slot, block, 2, (2,), False)
                advance(slot, block, 3, (3,), False)

                def more(j, carry):
                    advance(slot, block, j, (), False)
                    return carry

                lax.fori_loop(4, count, more, 0)

            @pl.when(block + 2 < blocks)
            def _():
                fetch(block + 2, (slot + 2) % IDS).start()

        return carry

    lax.fori_loop(0, blocks // IDS, four_blocks, 0)

    count = live(blocks - 1)
    added = contract(state[0])
    final = (IDS - 1) % 2
    totals[final] = jnp.where(count == 1, jnp.zeros_like(added), totals[final]) + added
    turn(IDS - 1)
    for slot in (IDS - 2, IDS - 1):
        fetch(0, slot).wait()
        place(slot, (0, 1, 2, 3))
    segment = segments(8)

    def close(group, carry):
        start = pl.multiple_of(group * 2048, 2048)
        dense = placed[pl.ds(start, LANES), :]
        for g in range(1, 16):
            part = placed[pl.ds(start + g * LANES, LANES), :]
            dense = jnp.where(segment == g, part, dense)
        flat = dense.T
        for g in range(16):
            result = flat[8 * g : 8 * g + 3] + flat[8 * g + 3 : 8 * g + 6]
            out_ref[:, pl.ds(start + g * LANES, LANES)] = result
        return carry

    lax.fori_loop(0, out_ref.shape[1] // 2048, close, 0)


def evaluate_rows(sent, order, points):
    nodes = points.shape[1]
    vmem = pl.BlockSpec(memory_space=pltpu.VMEM)
    return pl.pallas_call(
        evaluate_kernel,
        in_specs=[
            pl.BlockSpec(memory_space=pl.ANY),
            vmem,
            pl.BlockSpec(memory_space=pl.ANY),
        ],
        out_specs=vmem,
        out_shape=jax.ShapeDtypeStruct((3, nodes), F32),
        scratch_shapes=[
            pltpu.VMEM((nodes, LANES), F32),
            pltpu.VMEM((12, LANES, LANES), F32),
            pltpu.VMEM((192 * 24, LANES), F32),
            pltpu.VMEM((LANES, 512), F32),
            pltpu.VMEM((4, 2 * LANES, LANES), BF16),
            pltpu.VMEM((LANES, 32), BF16),
            pltpu.VMEM((2, 8, 512), F32),
            pltpu.VMEM((2, 512, LANES), F32),
            pltpu.VMEM((64, LANES), jnp.int32),
            pltpu.VMEM((8, LANES), jnp.int32),
            pltpu.SMEM((64, LANES), jnp.int32),
            pltpu.SMEM((8, LANES), jnp.int32),
            pltpu.SMEM((8,), jnp.int32),
        ]
        + [pltpu.SMEM((4, LANES), jnp.int32) for _ in range(IDS)]
        + [pltpu.SemaphoreType.DMA((IDS,)), pltpu.SemaphoreType.DMA((4,))]
        + [pltpu.VMEM(sent.shape, F32), pltpu.VMEM(points.shape, BF16)],
        compiler_params=pltpu.CompilerParams(vmem_limit_bytes=58 * 2**20),
        cost_estimate=pl.CostEstimate(flops=10**10, bytes_accessed=100 * 2**20, transcendentals=0),
        name="evaluate_rows",
    )(sent, order.reshape(-1, 4, LANES), points)


def pick(source, index):
    return jnp.take_along_axis(source, index, axis=1, mode="promise_in_bounds")


def pack_kernel(pos_ref, coef_ref, send_ref, cols_ref, count_ref, out_ref):
    slabs, sectors = 8, 16
    lane = lax.broadcasted_iota(jnp.int32, (1, LANES), 1)
    order = lax.broadcasted_iota(jnp.int32, (8, LANES), 0)
    surface = jnp.concatenate([pos_ref[...], coef_ref[...], coef_ref[0:2]], 0)
    wanted = 4 * lax.broadcasted_iota(jnp.int32, (8, LANES), 1) + (order & 3)
    sent = None
    for part in range(4):
        held = jnp.broadcast_to(send_ref[:, part * LANES : (part + 1) * LANES], (8, LANES))
        found = pick(held, wanted & (LANES - 1))
        sent = found if sent is None else jnp.where(wanted >> 7 == part, found, sent)
    picked = []
    for k in range(4):
        node = jnp.broadcast_to(sent[k : k + 1], (8, LANES))
        value = None
        for part in range(8):
            found = pick(surface[:, part * LANES : (part + 1) * LANES], node & (LANES - 1))
            value = found if value is None else jnp.where(node >> 7 == part, found, value)
        picked.append(value)
    low = jnp.concatenate([picked[k][c : c + 1] for c in range(3) for k in range(4)], 0)
    high = jnp.concatenate([picked[k][c : c + 1] for c in range(3, 6) for k in range(4)], 0)
    listed = jnp.where(order < count_ref[...], cols_ref[...], -1).astype(F32)
    lists = [pltpu.roll(listed, (48 - 8 * z) % LANES, 1) for z in range(sectors)]
    for a in range(slabs):
        base = min(max((a - 1) * sectors, 0), (slabs - 3) * sectors)
        left = low if base == 0 else pltpu.roll(low, LANES - base, 1)
        right = pltpu.roll(high, (64 - base) % LANES, 1)
        rows = jnp.where(lane < 64, left, right)
        for z in range(sectors):
            out_ref[a * sectors + z, 0:8, :] = jnp.where(lane // 8 == 6, lists[z], rows[0:8])
            out_ref[a * sectors + z, 8:12, :] = rows[8:12]
            out_ref[a * sectors + z, 12:16, :] = rows[8:12]


def pack(*operands):
    vmem = pl.BlockSpec(memory_space=pltpu.VMEM)
    return pl.pallas_call(
        pack_kernel,
        in_specs=[vmem] * 5,
        out_specs=vmem,
        out_shape=jax.ShapeDtypeStruct((LANES, 16, LANES), F32),
        name="pack",
    )(*operands)


def per_device(
    surface_pos, surface_coef, send_rows, volume_pos, relay_order, block_cols, block_count
):
    payload = pack(surface_pos, surface_coef, send_rows, block_cols.T, block_count[None])
    sent = lax.all_to_all(payload, ("axial", "azim"), split_axis=0, concat_axis=0, tiled=True)
    order = relay_order[0]
    points = gather_rows(order, volume_pos)
    return evaluate_rows(sent, order, points)


def solution(mesh):
    placed = (
        P(None, ("axial", "azim")),
        P(None, ("axial", "azim")),
        P(("axial", "azim"), None),
        P(None, ("axial", "azim")),
        P(("axial", "azim"), None),
        P(("axial", "azim"), None),
        P(("axial", "azim")),
    )
    return jax.shard_map(
        per_device,
        mesh=mesh,
        in_specs=placed,
        out_specs=P(None, ("axial", "azim")),
        check_vma=False,
    )
```
